32 devices in a mesh: groups: 2 (over x), tm: 16 (over z, y, core).
Axes of the slice: x: 2, y: 2, z: 4, core: 2. Of those that a mesh axis runs over, the one named last changes fastest.
Arguments:
- audio: bfloat16 [16777216], P(('groups', 'tm')), parts along dimension 0, may hold values from -6 to 6
- kernel: bfloat16 [2304, 1024], replicated, may hold values from -0.1875 to 0.1875
- templates: bfloat16 [1152, 512], replicated, may hold values from 0.005 to 0.7, as said below
- activations: bfloat16 [512, 32768], P(None, ('groups', 'tm')), parts along dimension 1, may hold values from 0.01 to 1, as said below
Outputs:
- new_activations: bfloat16 [512, 32768], P(None, ('groups', 'tm')), parts along dimension 1
- new_templates: bfloat16 [2304, 512], P('groups'), parts along dimension 0
The draws below stay inside these ranges and needn't reach their ends.
There are 2 independent parts, one for each index of `groups`. The reference program is written for one: setup_inputs(seed, part) draws one part's arguments, and reference() takes and returns one part's arrays. A program takes and returns all parts, laid end to end along the dimension named above; an argument that names none is the same for every part. Nothing has to cross between parts.
Inputs may be any that keep to these rules, and one draw needn't show every extreme that they name: `templates`: Positive. `activations`: Positive.
All inputs are finite; a program needn't handle non-finite values.
Results may differ from the reference program's by a relative error of at most 0.0051.
Values may be sent and summed in bfloat16 or wider, within the bound.
No kernel may reach another device: no remote copies, remote signals or barrier semaphores. Data moves between devices by JAX's collectives and lax.ppermute only.
A program may use at most 64 MiB of HBM per device.

```python
import math
import jax
import jax.numpy as jnp
from jax import lax

K = 1152
R = 512
HOP = 512
WIN = 1024
ITERS = 2
FRAMES = 1024
HALF = 256
FTOT = 16384
N_TM = 16


def draw_audio(key, part):
    key_noise, key_tilt = jax.random.split(key, 2)
    total = FRAMES * N_TM * HOP
    noise = jax.random.normal(key_noise, (total + 1,), jnp.float32)
    tilt = jax.random.uniform(key_tilt, (N_TM,), jnp.float32, 0.0, 0.85)
    block = jnp.arange(total, dtype=jnp.int32) // (FRAMES * HOP)
    blend = tilt[block]
    values = (noise[1:] + blend * noise[:-1]) / jnp.sqrt(1.0 + blend * blend)
    return jnp.clip(values, -6.0, 6.0).astype(jnp.bfloat16)


def draw_kernel(key, part):
    key_phase, key_amp, key_noise = jax.random.split(key, 3)
    bins = jnp.arange(K, dtype=jnp.float32)
    freq = 0.45 * jnp.exp2(-(K - 1.0 - bins) / 96.0)
    phase = jax.random.uniform(key_phase, (K,), jnp.float32, -math.pi, math.pi)
    amp = jnp.exp(jax.random.uniform(key_amp, (K,), jnp.float32, math.log(0.5), math.log(2.0)))
    place = jnp.arange(WIN, dtype=jnp.float32) + 0.5
    window = 0.5 - 0.5 * jnp.cos(2.0 * math.pi * place / WIN)
    turns = jnp.mod(freq[:, None] * place[None, :], 1.0)
    angle = 2.0 * math.pi * turns + phase[:, None]
    real_rows = amp[:, None] * window[None, :] * jnp.cos(angle)
    imag_rows = amp[:, None] * window[None, :] * jnp.sin(angle)
    noise = 0.2 * jnp.clip(jax.random.normal(key_noise, (2 * K, WIN), jnp.float32), -4.0, 4.0)
    values = (jnp.concatenate([real_rows, imag_rows], axis=0) + noise) / math.sqrt(0.3 * WIN)
    return values.astype(jnp.bfloat16)


def draw_templates(key, part):
    key_rough, key_slope = jax.random.split(key, 2)
    rough = jnp.exp(jax.random.uniform(key_rough, (K, R), jnp.float32, math.log(0.02), math.log(0.2)))
    slope = jax.random.uniform(key_slope, (1, R), jnp.float32, -2.5, 2.5)
    place = jnp.arange(K, dtype=jnp.float32)[:, None] / (K - 1.0) - 0.5
    values = rough * jnp.exp(slope * place)
    return values.astype(jnp.bfloat16)


def draw_activations(key, part):
    key_base, key_perm = jax.random.split(key, 2)
    total = FRAMES * N_TM
    base = jnp.exp(jax.random.uniform(key_base, (R, total), jnp.float32, math.log(0.01), math.log(0.1)))
    owner_of = jax.random.permutation(key_perm, N_TM)
    device = jnp.arange(total, dtype=jnp.int32) // FRAMES
    owner = owner_of[device]
    spiked = jnp.arange(R, dtype=jnp.int32)[:, None] % N_TM == owner[None, :]
    values = base * (1.0 + 9.0 * spiked.astype(jnp.float32))
    return values.astype(jnp.bfloat16)


def setup_inputs(seed: int = 0, part: int = 0) -> dict:
    keys = jax.random.split(jax.random.key(seed), 5)
    part_splits = jax.random.split(jax.random.fold_in(keys[4], part), 5)
    return {
        "audio": draw_audio(jax.random.fold_in(jax.random.fold_in(keys[4], part), 71), part),
        "kernel": draw_kernel(jax.random.fold_in(keys[4], 71), part),
        "templates": draw_templates(jax.random.fold_in(keys[4], 71), part),
        "activations": draw_activations(jax.random.fold_in(jax.random.fold_in(keys[4], part), 71), part),
    }


def spectrum(audio, kernel):
    padded = jnp.pad(audio, (HALF, HALF))
    blocks = padded.reshape(FTOT + 1, HOP)
    dims = (((1,), (1,)), ((), ()))
    spec = lax.dot_general(kernel[:, :HOP], blocks[:-1], dims, preferred_element_type=jnp.float32)
    spec = spec + lax.dot_general(kernel[:, HOP:], blocks[1:], dims, preferred_element_type=jnp.float32)
    return (spec[:K] * spec[:K] + spec[K:] * spec[K:]).astype(jnp.bfloat16)


def reference(audio, kernel, templates, activations):
    power = spectrum(audio, kernel).astype(jnp.float32)
    weights = templates
    acts = activations
    for step in range(ITERS):
        model = jnp.dot(weights, acts, preferred_element_type=jnp.float32)
        ratio = (power / model).astype(jnp.bfloat16)
        numer = lax.dot_general(weights, ratio, (((0,), (0,)), ((), ())), preferred_element_type=jnp.float32)
        colsum = jnp.sum(weights.astype(jnp.float32), axis=0)
        acts = (acts.astype(jnp.float32) * numer / colsum[:, None]).astype(jnp.bfloat16)
        model = jnp.dot(weights, acts, preferred_element_type=jnp.float32)
        ratio = (power / model).astype(jnp.bfloat16)
        numw = lax.dot_general(ratio, acts, (((1,), (1,)), ((), ())), preferred_element_type=jnp.float32)
        rowsum = jnp.sum(acts.astype(jnp.float32), axis=1)
        weights = (weights.astype(jnp.float32) * numw / rowsum[None, :]).astype(jnp.bfloat16)
    return acts, weights
```

```python
import jax
import jax.numpy as jnp
from jax import lax
from jax.sharding import PartitionSpec as P

HOP = 512
ITERS = 2
HALF = 256
HALVES = 2
bf16 = jnp.bfloat16
f32 = jnp.float32


def with_halo(x, axis, width):
    peers, length = lax.axis_size(axis), x.shape[0]
    up = [(i, (i + 1) % peers) for i in range(peers - 1)]
    down = [(j, i) for i, j in up]
    before = lax.ppermute(x[length - width :], axis, up)
    after = lax.ppermute(x[:width], axis, down)
    return jnp.concatenate([before, x, after], axis=0)


def exchanges(peers):
    me = lax.axis_index("tm")
    bits = [1 << b for b in range(peers.bit_length() - 1)]
    even = bits[:]
    odd = bits[:]
    if len(bits) > 2:
        odd[1], odd[2] = bits[2], bits[1]
    steps = []
    for e, o in zip(even, odd):
        bit = jnp.where(me % 2 == 0, (me // e) % 2, (me // o) % 2)
        steps.append((bit, [(i, i ^ (e if i % 2 == 0 else o)) for i in range(peers)]))
    return steps


def swap_totals(totals):
    hi = totals.astype(bf16)
    lo = (totals - hi.astype(f32)).astype(bf16)
    return hi, lo


def scatter_sum(cur, totals, steps, scattered):
    for number, (bit, perm) in enumerate(steps):
        if number < scattered:
            rows = cur.shape[0] // 2
            send = lax.dynamic_slice_in_dim(cur, (1 - bit) * rows, rows, 0).astype(bf16)
            cur = lax.dynamic_slice_in_dim(cur, bit * rows, rows, 0)
        else:
            rows = cur.shape[0]
            send = cur.astype(bf16)
            cur = send.astype(f32)
        if totals is not None:
            hi, lo = swap_totals(totals)
            pad = jnp.zeros((6, hi.shape[0]), bf16)
            send = jnp.concatenate([send, hi[None], lo[None], pad], axis=0)
        got = lax.ppermute(send, "tm", perm)
        cur = cur + got[:rows].astype(f32)
        if totals is not None:
            totals = (hi.astype(f32) + lo.astype(f32)) + (
                got[rows].astype(f32) + got[rows + 1].astype(f32)
            )
    return cur, totals


def gather(part, steps, scattered):
    for bit, perm in reversed(steps[:scattered]):
        got = lax.ppermute(part, "tm", perm)
        part = jnp.where(
            bit == 0,
            jnp.concatenate([part, got], axis=0),
            jnp.concatenate([got, part], axis=0),
        )
    return part


def on_device(audio, kernel, templates, activations):
    peers = lax.axis_size("tm")
    padded = with_halo(audio, "tm", HALF)
    frames = activations.shape[1]
    blocks = padded.reshape(frames + 1, HOP)
    dims = (((1,), (1,)), ((), ()))
    spec = lax.dot_general(kernel[:, :HOP], blocks[:-1], dims, preferred_element_type=f32)
    spec = spec + lax.dot_general(kernel[:, HOP:], blocks[1:], dims, preferred_element_type=f32)
    bins = templates.shape[0]
    power = (spec[:bins] * spec[:bins] + spec[bins:] * spec[bins:]).astype(bf16).astype(f32)
    part = bins // HALVES
    powers = [power[i * part : (i + 1) * part] for i in range(HALVES)]
    weights = [templates[i * part : (i + 1) * part] for i in range(HALVES)]
    steps = exchanges(peers)
    scattered = min(3, len(steps))
    acts = activations
    for step in range(ITERS):
        numer = 0.0
        colsum = 0.0
        for w, p in zip(weights, powers):
            model = jnp.dot(w, acts, preferred_element_type=f32)
            ratio = (p / model).astype(bf16)
            numer = numer + lax.dot_general(
                w, ratio, (((0,), (0,)), ((), ())), preferred_element_type=f32
            )
            colsum = colsum + jnp.sum(w.astype(f32), axis=0)
        acts = (acts.astype(f32) * numer / colsum[:, None]).astype(bf16)
        totals = jnp.sum(acts.astype(f32), axis=1)
        news = []
        for i, (w, p) in enumerate(zip(weights, powers)):
            model = jnp.dot(w, acts, preferred_element_type=f32)
            ratio = (p / model).astype(bf16)
            numw = lax.dot_general(ratio, acts, (((1,), (1,)), ((), ())), preferred_element_type=f32)
            numw, sums = scatter_sum(numw, totals if i == 0 else None, steps, scattered)
            if i == 0:
                rowsum = sums
            own = w
            for bit, _ in steps[:scattered]:
                rows = own.shape[0] // 2
                own = lax.dynamic_slice_in_dim(own, bit * rows, rows, 0)
            own = (own.astype(f32) * numw / rowsum[None, :]).astype(bf16)
            news.append(gather(own, steps, scattered))
        weights = news
    return (acts, jnp.concatenate(weights, axis=0))


def solution(mesh):
    in_specs = (P(("groups", "tm")), P(), P(), P(None, ("groups", "tm")))
    out_specs = (P(None, ("groups", "tm")), P("groups", None))
    return jax.shard_map(
        on_device, mesh=mesh, in_specs=in_specs, out_specs=out_specs, check_vma=False
    )
```

```python
import functools

import jax
import jax.numpy as jnp
from jax import lax
from jax.experimental import pallas as pl
from jax.experimental.pallas import tpu as pltpu
from jax.sharding import PartitionSpec as P

HOP = 512
ITERS = 2
HALF = 256
TILE = 256
bf16 = jnp.bfloat16
f32 = jnp.float32
NT = (((1,), (1,)), ((), ()))


def inverse(x):
    r = pl.reciprocal(x, approx=True)
    return r * (2.0 - x * r)


def dot(a, b):
    return jnp.dot(a, b, preferred_element_type=f32)


def dot_nt(a, b):
    return lax.dot_general(a, b, NT, preferred_element_type=f32)


def row_blocks(rows):
    first = rows % TILE
    cuts = [0] + list(range(first + TILE if first else TILE, rows + 1, TILE))
    return list(zip(cuts[:-1], cuts[1:]))


def analyse_kernel(bins, cut, a_ref, halo_ref, k_ref, w_ref, h_ref, pa_ref, pb_ref, new_ref,
                   wide, frame, wt):
    frames = a_ref.shape[0]
    wide[8 : 8 + frames, :] = a_ref[...].astype(f32)
    wide[7:8, HALF:] = halo_ref[0:1, :]
    wide[8 + frames : 9 + frames, :HALF] = halo_ref[1:2, :]
    frame[:, HALF : HALF + HOP] = a_ref[...]
    frame[:, :HALF] = wide[7 : 7 + frames, HALF:].astype(bf16)
    frame[:, HALF + HOP :] = wide[9 : 9 + frames, :HALF].astype(bf16)
    wt[...] = w_ref[...].T
    inv = inverse(jnp.sum(wt[...].astype(f32), axis=1, keepdims=True))

    def body(i, _):
        tile = pl.ds(pl.multiple_of(i * TILE, TILE), TILE)
        f = frame[tile, :]
        h = h_ref[:, tile]
        numer = None
        for lo, hi in row_blocks(bins):
            re = dot_nt(k_ref[lo:hi, :], f)
            im = dot_nt(k_ref[bins + lo : bins + hi, :], f)
            p = (re * re + im * im).astype(bf16)
            if hi <= cut:
                pa_ref[lo:hi, tile] = p
            else:
                pb_ref[lo - cut : hi - cut, tile] = p
            model = dot(w_ref[lo:hi, :], h)
            ratio = (p.astype(f32) * inverse(model)).astype(bf16)
            part = dot(wt[:, lo:hi], ratio)
            numer = part if numer is None else numer + part
        new_ref[:, tile] = (h.astype(f32) * numer * inv).astype(bf16)
        return 0

    lax.fori_loop(0, frames // TILE, body, 0)


def template_kernel(p_ref, w_ref, h_ref, numw_ref, *tot_ref):
    frames = h_ref.shape[1]
    for lo, hi in row_blocks(p_ref.shape[0]):
        acc = None
        for t in range(0, frames, TILE):
            h = h_ref[:, t : t + TILE]
            model = dot(w_ref[lo:hi, :], h)
            ratio = (p_ref[lo:hi, t : t + TILE].astype(f32) * inverse(model)).astype(bf16)
            part = dot_nt(ratio, h)
            acc = part if acc is None else acc + part
        numw_ref[lo:hi, :] = acc
    if tot_ref:
        ones = jnp.ones((16, frames), bf16)
        tot_ref[0][...] = dot_nt(ones, h_ref[...])[:8]


def activation_kernel(first, p_ref, w_ref, h_ref, *refs):
    if first:
        numer_ref, col_ref, wt = refs
    else:
        old_ref, oldcol_ref, new_ref, wt = refs
    frames = h_ref.shape[1]
    wt[...] = w_ref[...].T
    col = jnp.sum(wt[...].astype(f32), axis=1, keepdims=True)
    if first:
        col_ref[...] = jnp.broadcast_to(col, col_ref.shape)
    else:
        inv = inverse(col + oldcol_ref[:, :1])
    for t in range(0, frames, TILE):
        tile = slice(t, t + TILE)
        h = h_ref[:, tile]
        numer = None if first else old_ref[:, tile]
        for lo, hi in row_blocks(p_ref.shape[0]):
            model = dot(w_ref[lo:hi, :], h)
            ratio = (p_ref[lo:hi, tile].astype(f32) * inverse(model)).astype(bf16)
            part = dot(wt[:, lo:hi], ratio)
            numer = part if numer is None else numer + part
        if first:
            numer_ref[:, tile] = numer
        else:
            new_ref[:, tile] = (h.astype(f32) * numer * inv).astype(bf16)


VMEM = pl.BlockSpec(memory_space=pltpu.VMEM)


def call(kernel, outs, scratch, flops, *args):
    size = sum(a.size * a.dtype.itemsize for a in args)
    size += sum(o.size * o.dtype.itemsize for o in outs)
    return pl.pallas_call(
        kernel,
        out_shape=tuple(outs),
        in_specs=[VMEM] * len(args),
        out_specs=tuple([VMEM] * len(outs)),
        scratch_shapes=scratch,
        cost_estimate=pl.CostEstimate(flops=flops, bytes_accessed=size, transcendentals=0),
        compiler_params=pltpu.CompilerParams(vmem_limit_bytes=40 * 1024 * 1024),
    )(*args)


def shape(dims, dtype):
    return jax.ShapeDtypeStruct(dims, dtype)


def analyse(audio, halo, kernel, weights, acts, cut):
    bins, comps = weights.shape
    frames = acts.shape[1]
    return call(
        functools.partial(analyse_kernel, bins, cut),
        [shape((cut, frames), bf16), shape((bins - cut, frames), bf16), shape((comps, frames), bf16)],
        [
            pltpu.VMEM((frames + 16, HOP), f32),
            pltpu.VMEM((frames, 2 * HOP), bf16),
            pltpu.VMEM((comps, bins), bf16),
        ],
        2 * bins * frames * (4 * HOP + 2 * comps),
        audio, halo, kernel, weights, acts,
    )


def template_numerator(power, weights, acts, with_totals):
    bins, comps = weights.shape
    outs = [shape((bins, comps), f32)] + ([shape((8, comps), f32)] if with_totals else [])
    return call(template_kernel, outs, [], 4 * power.size * comps, power, weights, acts)


def activation_numerator(power, weights, acts):
    bins, comps = weights.shape
    return call(
        functools.partial(activation_kernel, True),
        [shape(acts.shape, f32), shape((comps, 128), f32)],
        [pltpu.VMEM((comps, bins), bf16)],
        4 * power.size * comps, power, weights, acts,
    )


def new_activations(power, weights, acts, numer, colsum):
    bins, comps = weights.shape
    return call(
        functools.partial(activation_kernel, False),
        [shape(acts.shape, bf16)],
        [pltpu.VMEM((comps, bins), bf16)],
        4 * power.size * comps, power, weights, acts, numer, colsum,
    )[0]


def halo_rows(audio, peers):
    me = lax.axis_index("tm")
    odd = me % 2 == 1
    head, tail = audio[:HALF], audio[audio.shape[0] - HALF :]
    inner = [(i, i ^ 1) for i in range(peers)]
    outer = [(i, (i + 1) % peers if i % 2 else (i - 1) % peers) for i in range(peers)]
    one = lax.ppermute(jnp.where(odd, head, tail), "tm", inner)
    two = lax.ppermute(jnp.where(odd, tail, head), "tm", outer)
    zero = jnp.zeros_like(two)
    two = jnp.where((me == 0) | (me == peers - 1), zero, two)
    left = jnp.where(odd, one, two)
    right = jnp.where(odd, two, one)
    return jnp.stack([left, right]).astype(f32)


def exchanges(peers):
    me = lax.axis_index("tm")
    even = [1 << b for b in range(peers.bit_length() - 1)]
    odd = even[:]
    if len(even) > 2:
        odd[1], odd[2] = even[2], even[1]
    steps = []
    for e, o in zip(even, odd):
        bit = jnp.where(me % 2 == 0, (me // e) % 2, (me // o) % 2)
        steps.append((bit, [(i, i ^ (e if i % 2 == 0 else o)) for i in range(peers)]))
    return steps


def scatter_sum(cur, totals, steps, scattered):
    for number, (bit, perm) in enumerate(steps):
        if number < scattered:
            rows = cur.shape[0] // 2
            send = lax.dynamic_slice_in_dim(cur, (1 - bit) * rows, rows, 0).astype(bf16)
            cur = lax.dynamic_slice_in_dim(cur, bit * rows, rows, 0)
        else:
            rows = cur.shape[0]
            send = cur.astype(bf16)
            cur = send.astype(f32)
        if totals is not None:
            hi = totals.astype(bf16)
            lo = (totals - hi.astype(f32)).astype(bf16)
            pad = jnp.zeros((6, hi.shape[0]), bf16)
            send = jnp.concatenate([send, hi[None], lo[None], pad], axis=0)
        got = lax.ppermute(send, "tm", perm)
        cur = cur + got[:rows].astype(f32)
        if totals is not None:
            totals = (hi.astype(f32) + lo.astype(f32)) + (
                got[rows].astype(f32) + got[rows + 1].astype(f32)
            )
    return cur, totals


def gather(part, steps, scattered):
    for bit, perm in reversed(steps[:scattered]):
        got = lax.ppermute(part, "tm", perm)
        part = jnp.where(
            bit == 0,
            jnp.concatenate([part, got], axis=0),
            jnp.concatenate([got, part], axis=0),
        )
    return part


def on_device(audio, kernel, templates, activations):
    peers = lax.axis_size("tm")
    frames = activations.shape[1]
    bins = templates.shape[0]
    cut = bins // 2 // 128 * 128 + 128
    halo = halo_rows(audio, peers)
    *powers, acts = analyse(
        audio.reshape(frames, HOP), halo, kernel, templates, activations, cut
    )
    weights = [templates[:cut], templates[cut:]]
    steps = exchanges(peers)
    scattered = min(3, len(steps))
    for step in range(ITERS):
        if step:
            numer, colsum = activation_numerator(powers[0], weights[0], acts)
            acts = new_activations(powers[1], weights[1], acts, numer, colsum)
        news = []
        for i, (w, p) in enumerate(zip(weights, powers)):
            numw, *totals = template_numerator(p, w, acts, i == 0)
            numw, sums = scatter_sum(numw, totals[0][0] if totals else None, steps, scattered)
            if i == 0:
                rowsum = sums
            own = w
            for bit, _ in steps[:scattered]:
                rows = own.shape[0] // 2
                own = lax.dynamic_slice_in_dim(own, bit * rows, rows, 0)
            own = (own.astype(f32) * numw / rowsum[None, :]).astype(bf16)
            news.append(gather(own, steps, scattered))
        weights = news
    return (acts, jnp.concatenate(weights, axis=0))


def solution(mesh):
    in_specs = (P(("groups", "tm")), P(), P(), P(None, ("groups", "tm")))
    out_specs = (P(None, ("groups", "tm")), P("groups", None))
    return jax.shard_map(
        on_device, mesh=mesh, in_specs=in_specs, out_specs=out_specs, check_vma=False
    )
```

```python
import functools

import jax
import jax.numpy as jnp
from jax import lax
from jax.experimental import pallas as pl
from jax.experimental.pallas import tpu as pltpu
from jax.sharding import PartitionSpec as P

HOP = 512
ITERS = 2
HALF = 256
TILE = 256
LANES = 128
bf16 = jnp.bfloat16
f32 = jnp.float32
NT = (((1,), (1,)), ((), ()))


def inverse(x):
    r = pl.reciprocal(x, approx=True)
    return r * (2.0 - x * r)


def dot(a, b):
    return jnp.dot(a, b, preferred_element_type=f32)


def dot_nt(a, b):
    return lax.dot_general(a, b, NT, preferred_element_type=f32)


def row_blocks(rows):
    first = rows % TILE
    cuts = [0] + list(range(first + TILE if first else TILE, rows + 1, TILE))
    return list(zip(cuts[:-1], cuts[1:]))


def analyse_kernel(cut, halo_ref, a_hbm, k_hbm, w_hbm, h_hbm, pa_ref, pb_ref, new_ref,
                   a_ref, k_ref, w_ref, h_ref, wide, frame, wt, a_sem, k_sem, w_sem, h_sem):
    bins = w_ref.shape[0]
    frames = h_ref.shape[1]
    blocks = row_blocks(bins)
    a_copy = pltpu.make_async_copy(a_hbm, a_ref, a_sem)
    a_copy.start()
    k_copies = []
    for n, (lo, hi) in enumerate(blocks):
        pair = []
        for m, base in enumerate((0, bins)):
            rows = pl.ds(base + lo, hi - lo)
            pair.append(pltpu.make_async_copy(k_hbm.at[rows], k_ref.at[rows], k_sem.at[2 * n + m]))
            pair[-1].start()
        k_copies.append(pair)
    w_copy = pltpu.make_async_copy(w_hbm, w_ref, w_sem)
    h_copy = pltpu.make_async_copy(h_hbm, h_ref, h_sem)
    w_copy.start()
    h_copy.start()

    a_copy.wait()
    wide[8 : 8 + a_ref.shape[0], :] = a_ref[...].astype(f32)
    wide[6:8, :] = halo_ref[0:2, :]
    wide[8 + a_ref.shape[0] : 10 + a_ref.shape[0], :] = halo_ref[2:4, :]
    for j in range(2 * HOP // LANES):
        rows = wide[pl.ds(6 + j, frames, stride=HOP // LANES), :]
        frame[:, j * LANES : (j + 1) * LANES] = rows.astype(bf16)

    for (lo, hi), pair in zip(blocks, k_copies):
        for copy in pair:
            copy.wait()
        for t in range(0, frames, TILE):
            f = frame[t : t + TILE, :]
            re = dot_nt(k_ref[lo:hi, :], f)
            im = dot_nt(k_ref[bins + lo : bins + hi, :], f)
            p = (re * re + im * im).astype(bf16)
            if hi <= cut:
                pa_ref[lo:hi, t : t + TILE] = p
            else:
                pb_ref[lo - cut : hi - cut, t : t + TILE] = p

    w_copy.wait()
    h_copy.wait()
    wt[...] = w_ref[...].T
    inv = inverse(jnp.sum(wt[...].astype(f32), axis=1, keepdims=True))
    for t in range(0, frames, TILE):
        tile = slice(t, t + TILE)
        h = h_ref[:, tile]
        numer = None
        for lo, hi in blocks:
            p = pa_ref[lo:hi, tile] if hi <= cut else pb_ref[lo - cut : hi - cut, tile]
            model = dot(w_ref[lo:hi, :], h)
            ratio = (p.astype(f32) * inverse(model)).astype(bf16)
            part = dot(wt[:, lo:hi], ratio)
            numer = part if numer is None else numer + part
        new_ref[:, tile] = (h.astype(f32) * numer * inv).astype(bf16)


def template_kernel(send, base, extras, at_ref, p_ref, w_ref, h_ref, *outs):
    frames = h_ref.shape[1]
    outs = list(outs)
    numw_ref = outs.pop(0)
    rows = p_ref.shape[0] // 2
    own = pl.multiple_of(at_ref[0] * rows, 16)
    w = w_ref[pl.ds(base + own, rows), :]
    for lo, hi in row_blocks(rows):
        acc = None
        for t in range(0, frames, TILE):
            h = h_ref[:, t : t + TILE]
            model = dot(w[lo:hi, :], h)
            p = p_ref[pl.ds(own + lo, hi - lo), t : t + TILE]
            ratio = (p.astype(f32) * inverse(model)).astype(bf16)
            part = dot_nt(ratio, h)
            acc = part if acc is None else acc + part
        numw_ref[lo:hi, :] = acc.astype(numw_ref.dtype)
    if "totals" in extras:
        total = dot_nt(jnp.ones((16, frames), bf16), h_ref[...])
        high = total.astype(bf16).astype(f32)
        low = (total - high).astype(bf16).astype(f32)
        if send:
            row = lax.broadcasted_iota(jnp.int32, total.shape, 0)
            both = jnp.where(row == 0, high, jnp.where(row == 1, low, 0.0))
            numw_ref[rows : rows + 16, :] = both.astype(bf16)
        else:
            outs.pop(0)[...] = (high + low)[:8]
    if not send:
        outs.pop(0)[...] = w
    if "copy" in extras:
        outs.pop(0)[...] = h_ref[...]


def activation_kernel(first, p_ref, w_ref, h_ref, *refs):
    if first:
        numer_ref, col_ref, wt = refs
    else:
        old_ref, oldcol_ref, new_ref, wt = refs
    frames = h_ref.shape[1]
    wt[...] = w_ref[...].T
    col = jnp.sum(wt[...].astype(f32), axis=1, keepdims=True)
    if first:
        col_ref[...] = jnp.broadcast_to(col, col_ref.shape)
    else:
        inv = inverse(col + oldcol_ref[:, :1])
    for t in range(0, frames, TILE):
        tile = slice(t, t + TILE)
        h = h_ref[:, tile]
        numer = None if first else old_ref[:, tile]
        for lo, hi in row_blocks(p_ref.shape[0]):
            model = dot(w_ref[lo:hi, :], h)
            ratio = (p_ref[lo:hi, tile].astype(f32) * inverse(model)).astype(bf16)
            part = dot(wt[:, lo:hi], ratio)
            numer = part if numer is None else numer + part
        if first:
            numer_ref[:, tile] = numer
        else:
            new_ref[:, tile] = (h.astype(f32) * numer * inv).astype(bf16)


VMEM = pl.BlockSpec(memory_space=pltpu.VMEM)
HBM = pl.BlockSpec(memory_space=pltpu.HBM)


def call(kernel, outs, scratch, flops, *args, specs=None, mib=16):
    size = sum(a.size * a.dtype.itemsize for a in args)
    size += sum(o.size * o.dtype.itemsize for o in outs)
    return pl.pallas_call(
        kernel,
        out_shape=tuple(outs),
        in_specs=specs or [VMEM] * len(args),
        out_specs=tuple([VMEM] * len(outs)),
        scratch_shapes=scratch,
        cost_estimate=pl.CostEstimate(flops=flops*100, bytes_accessed=size*100, transcendentals=0),
        compiler_params=pltpu.CompilerParams(vmem_limit_bytes=mib * 1024 * 1024),
    )(*args)


def shape(dims, dtype):
    return jax.ShapeDtypeStruct(dims, dtype)


def analyse(audio, halo, kernel, weights, acts, cut):
    bins, comps = weights.shape
    frames = acts.shape[1]
    blocks = len(row_blocks(bins))
    return call(
        functools.partial(analyse_kernel, cut),
        [shape((cut, frames), bf16), shape((bins - cut, frames), bf16), shape((comps, frames), bf16)],
        [
            pltpu.VMEM(audio.shape, bf16),
            pltpu.VMEM(kernel.shape, bf16),
            pltpu.VMEM(weights.shape, bf16),
            pltpu.VMEM(acts.shape, bf16),
            pltpu.VMEM((audio.shape[0] + 16, LANES), f32),
            pltpu.VMEM((frames, 2 * HOP), bf16),
            pltpu.VMEM((comps, bins), bf16),
            pltpu.SemaphoreType.DMA,
            pltpu.SemaphoreType.DMA((2 * blocks,)),
            pltpu.SemaphoreType.DMA,
            pltpu.SemaphoreType.DMA,
        ],
        2 * bins * frames * (4 * HOP + 2 * comps),
        halo, *[pltpu.with_memory_space_constraint(x, pltpu.HBM) for x in (audio, kernel, weights, acts)],
        specs=[VMEM, HBM, HBM, HBM, HBM],
        mib=32,
    )


def template_numerator(send, at, power, weights, base, acts, extras=()):
    rows, comps = power.shape[0] // 2, acts.shape[0]
    if send:
        outs = [shape((rows + (16 if "totals" in extras else 0), comps), bf16)]
    else:
        outs = [shape((rows, comps), f32)]
        if "totals" in extras:
            outs.append(shape((8, comps), f32))
        outs.append(shape((rows, comps), bf16))
    if "copy" in extras:
        outs.append(shape(acts.shape, bf16))
    kernel = functools.partial(template_kernel, send, base, extras)
    at = jnp.reshape(1 - at if send else at, (1,)).astype(jnp.int32)
    return call(
        kernel, outs, [], 2 * power.size * comps, at, power, weights, acts,
        specs=[pl.BlockSpec(memory_space=pltpu.SMEM)] + [VMEM] * 3,
    )


def activation_numerator(power, weights, acts):
    bins, comps = weights.shape
    return call(
        functools.partial(activation_kernel, True),
        [shape(acts.shape, f32), shape((comps, 128), f32)],
        [pltpu.VMEM((comps, bins), bf16)],
        4 * power.size * comps, power, weights, acts,
    )


def new_activations(power, weights, acts, numer, colsum):
    bins, comps = weights.shape
    return call(
        functools.partial(activation_kernel, False),
        [shape(acts.shape, bf16)],
        [pltpu.VMEM((comps, bins), bf16)],
        4 * power.size * comps, power, weights, acts, numer, colsum,
    )[0]


def halo_rows(audio, peers):
    me = lax.axis_index("tm")
    odd = me % 2 == 1
    rows = HALF // LANES
    head, tail = audio[:rows], audio[audio.shape[0] - rows :]
    inner = [(i, i ^ 1) for i in range(peers)]
    outer = [(i, (i + 1) % peers if i % 2 else (i - 1) % peers) for i in range(peers)]
    one = lax.ppermute(jnp.where(odd, head, tail), "tm", inner)
    two = lax.ppermute(jnp.where(odd, tail, head), "tm", outer)
    two = jnp.where((me == 0) | (me == peers - 1), jnp.zeros_like(two), two)
    left = jnp.where(odd, one, two)
    right = jnp.where(odd, two, one)
    return jnp.concatenate([left, right], axis=0).astype(f32)


class Group:
    def __init__(self, bits, peers):
        me = lax.axis_index("tm")
        self.size = 1 << len(bits)
        self.me = sum(((me // b) % 2) << j for j, b in enumerate(bits))
        self.others = []
        for code in range(1, self.size):
            mask = sum(b for j, b in enumerate(bits) if code >> j & 1)
            self.others.append((code, [(i, i ^ mask) for i in range(peers)]))


def groups_of(peers):
    bits = [1 << b for b in range(peers.bit_length() - 1)]
    shared = [Group(g, peers) for g in (bits[:1], bits[1:3]) if g]
    return shared, [Group([b], peers) for b in bits[3:]]


def block_of(x, index, rows):
    return lax.dynamic_slice_in_dim(x, index * rows, rows, 0)


def swap(send, totals, perm):
    rows = send.shape[0]
    if totals is None:
        return lax.ppermute(send, "tm", perm).astype(f32), None
    hi, lo = totals
    pad = jnp.zeros((6, hi.shape[0]), bf16)
    got = lax.ppermute(jnp.concatenate([send, hi[None], lo[None], pad], axis=0), "tm", perm)
    return got[:rows].astype(f32), got[rows].astype(f32) + got[rows + 1].astype(f32)


def share_out(cur, totals, group):
    rows = cur.shape[0] // group.size
    halves = None
    if totals is not None:
        hi = totals.astype(bf16)
        halves = (hi, (totals - hi.astype(f32)).astype(bf16))
        totals = halves[0].astype(f32) + halves[1].astype(f32)
    own = block_of(cur, group.me, rows)
    for code, perm in group.others:
        got, more = swap(block_of(cur, group.me ^ code, rows).astype(bf16), halves, perm)
        own = own + got
        if totals is not None:
            totals = totals + more
    return own, totals


def sum_pair(cur, totals, group):
    halves = None
    send = cur.astype(bf16)
    if totals is not None:
        hi = totals.astype(bf16)
        halves = (hi, (totals - hi.astype(f32)).astype(bf16))
        totals = halves[0].astype(f32) + halves[1].astype(f32)
    got, more = swap(send, halves, group.others[0][1])
    return send.astype(f32) + got, None if totals is None else totals + more


def gather(part, group):
    rows = part.shape[0]
    out = jnp.zeros((rows * group.size,) + part.shape[1:], part.dtype)
    out = lax.dynamic_update_slice_in_dim(out, part, group.me * rows, 0)
    for code, perm in group.others:
        got = lax.ppermute(part, "tm", perm)
        out = lax.dynamic_update_slice_in_dim(out, got, (group.me ^ code) * rows, 0)
    return out


def on_device(audio, kernel, templates, activations):
    peers = lax.axis_size("tm")
    frames = activations.shape[1]
    bins = templates.shape[0]
    cut = bins // 2 // 128 * 128 + 128
    audio = audio.reshape(audio.shape[0] // LANES, LANES)
    halo = halo_rows(audio, peers)
    *powers, acts = analyse(audio, halo, kernel, templates, activations, cut)
    weights = [(templates, 0), (templates, cut)]
    shared, pairs = groups_of(peers)
    core, rest = shared[0], shared[1:]
    for step in range(ITERS):
        last = step == ITERS - 1
        totals, parts = None, []
        for i, ((w, base), p) in enumerate(zip(weights, powers)):
            with_totals = ("totals",) if i == 0 else ()
            (send,) = template_numerator(True, core.me, p, w, base, acts, with_totals)
            got = lax.ppermute(send, "tm", core.others[0][1])
            extras = with_totals + (("copy",) if i == 1 and last else ())
            own, *more = template_numerator(False, core.me, p, w, base, acts, extras)
            rows = own.shape[0]
            own = own + got[:rows].astype(f32)
            tot = None
            if i == 0:
                tot = more.pop(0)[0] + (got[rows].astype(f32) + got[rows + 1].astype(f32))
            mine = more.pop(0)
            if more:
                final_acts = more.pop(0)
            for group in rest:
                own, tot = share_out(own, tot, group)
                mine = block_of(mine, group.me, mine.shape[0] // group.size)
            for group in pairs:
                own, tot = sum_pair(own, tot, group)
            if i == 0:
                totals = tot
            part = (mine.astype(f32) * own / totals[None, :]).astype(bf16)
            for group in reversed(rest):
                part = gather(part, group)
            parts.append(part)
        first, second = [gather(part, core) for part in parts]
        if last:
            return (final_acts, jnp.concatenate([first, second], axis=0))
        numer, colsum = activation_numerator(powers[0], first, acts)
        acts = new_activations(powers[1], second, acts, numer, colsum)
        weights = [(first, 0), (second, 0)]


def solution(mesh):
    in_specs = (P(("groups", "tm")), P(), P(), P(None, ("groups", "tm")))
    out_specs = (P(None, ("groups", "tm")), P("groups", None))
    return jax.shard_map(
        on_device, mesh=mesh, in_specs=in_specs, out_specs=out_specs, check_vma=False
    )
```

```python
import functools

import jax
import jax.numpy as jnp
from jax import lax
from jax.experimental import pallas as pl
from jax.experimental.pallas import tpu as pltpu
from jax.sharding import PartitionSpec as P

HOP = 512
ITERS = 2
HALF = 256
TILE = 256
LANES = 128
bf16 = jnp.bfloat16
f32 = jnp.float32
DIRECT = ((False, True), (True, False))
NT = (((1,), (1,)), ((), ()))


def inverse(x):
    r = pl.reciprocal(x, approx=True)
    return r * (2.0 - x * r)


def dot(a, b):
    return jnp.dot(a, b, preferred_element_type=f32)


def dot_nt(a, b):
    return lax.dot_general(a, b, NT, preferred_element_type=f32)


def row_blocks(rows):
    if rows < TILE:
        return [(0, rows)]
    first = rows % TILE
    cuts = [0] + list(range(first + TILE if first else TILE, rows + 1, TILE))
    return list(zip(cuts[:-1], cuts[1:]))


def analyse_kernel(rows, at_ref, halo_ref, a_hbm, k_hbm, w_hbm, h_hbm, p_ref, new_ref, w_ref,
                   a_ref, k_ref, h_ref, wide, frame, wt, a_sem, k_sem, w_sem, h_sem):
    bins = w_ref.shape[0]
    frames = h_ref.shape[1]
    blocks = row_blocks(bins)
    a_copy = pltpu.make_async_copy(a_hbm, a_ref, a_sem)
    a_copy.start()
    k_copies, w_copies = [], []
    for n in range(bins // rows):
        start = pl.multiple_of(at_ref[n] * rows, 16)
        here = pl.ds(n * rows, rows)
        for m in range(2):
            k_copies.append(
                pltpu.make_async_copy(
                    k_hbm.at[pl.ds(m * bins + start, rows)],
                    k_ref.at[pl.ds(m * bins + n * rows, rows)],
                    k_sem.at[2 * n + m],
                )
            )
        w_copies.append(pltpu.make_async_copy(w_hbm.at[pl.ds(start, rows)], w_ref.at[here], w_sem.at[n]))
    h_copy = pltpu.make_async_copy(h_hbm, h_ref, h_sem)
    for copy in k_copies + w_copies + [h_copy]:
        copy.start()

    a_copy.wait()
    wide[8 : 8 + a_ref.shape[0], :] = a_ref[...].astype(f32)
    wide[6:8, :] = halo_ref[0:2, :]
    wide[8 + a_ref.shape[0] : 10 + a_ref.shape[0], :] = halo_ref[2:4, :]
    for j in range(2 * HOP // LANES):
        strip = wide[pl.ds(6 + j, frames, stride=HOP // LANES), :]
        frame[:, j * LANES : (j + 1) * LANES] = strip.astype(bf16)

    waited = 0
    for lo, hi in blocks:
        while waited < -(-hi // rows):
            k_copies[2 * waited].wait()
            k_copies[2 * waited + 1].wait()
            waited += 1
        for t in range(0, frames, TILE):
            f = frame[t : t + TILE, :]
            re = dot_nt(k_ref[lo:hi, :], f)
            im = dot_nt(k_ref[bins + lo : bins + hi, :], f)
            p_ref[lo:hi, t : t + TILE] = (re * re + im * im).astype(bf16)

    for copy in w_copies + [h_copy]:
        copy.wait()
    wt[...] = w_ref[...].T
    inv = inverse(jnp.sum(wt[...].astype(f32), axis=1, keepdims=True))
    for t in range(0, frames, TILE):
        tile = slice(t, t + TILE)
        h = h_ref[:, tile]
        numer = None
        for lo, hi in blocks:
            model = dot(w_ref[lo:hi, :], h)
            ratio = (p_ref[lo:hi, tile].astype(f32) * inverse(model)).astype(bf16)
            part = dot(wt[:, lo:hi], ratio)
            numer = part if numer is None else numer + part
        new_ref[:, tile] = (h.astype(f32) * numer * inv).astype(bf16)


def template_kernel(size, p_base, w_base, extras, p_ref, w_ref, h_ref, *outs):
    frames = h_ref.shape[1]
    outs = list(outs)
    numw_ref = outs.pop(0)
    for lo, hi in row_blocks(size):
        w = w_ref[w_base + lo : w_base + hi, :]
        acc = None
        for t in range(0, frames, TILE):
            h = h_ref[:, t : t + TILE]
            model = dot(w, h)
            p = p_ref[p_base + lo : p_base + hi, t : t + TILE]
            ratio = (p.astype(f32) * inverse(model)).astype(bf16)
            part = dot_nt(ratio, h)
            acc = part if acc is None else acc + part
        numw_ref[lo:hi, :] = acc.astype(numw_ref.dtype)
    if "send" in extras or "totals" in extras:
        total = dot_nt(jnp.ones((16, frames), bf16), h_ref[...])
        high = total.astype(bf16).astype(f32)
        low = (total - high).astype(bf16).astype(f32)
        if "send" in extras:
            row = lax.broadcasted_iota(jnp.int32, total.shape, 0)
            both = jnp.where(row == 0, high, jnp.where(row == 1, low, 0.0))
            numw_ref[size : size + 16, :] = both.astype(bf16)
        else:
            outs.pop(0)[...] = (high + low)[:8]
    if "templates" in extras:
        outs.pop(0)[...] = w_ref[w_base : w_base + size, :]
    if "copy" in extras:
        outs.pop(0)[...] = h_ref[...]


def activation_kernel(first, base, p_ref, w_ref, h_ref, *refs):
    if first:
        numer_ref, col_ref, wt = refs
    else:
        old_ref, oldcol_ref, new_ref, wt = refs
    frames = h_ref.shape[1]
    wt[...] = w_ref[...].T
    col = jnp.sum(wt[...].astype(f32), axis=1, keepdims=True)
    if first:
        col_ref[...] = jnp.broadcast_to(col, col_ref.shape)
    else:
        inv = inverse(col + oldcol_ref[:, :1])
    for t in range(0, frames, TILE):
        tile = slice(t, t + TILE)
        h = h_ref[:, tile]
        numer = None if first else old_ref[:, tile]
        for lo, hi in row_blocks(w_ref.shape[0]):
            model = dot(w_ref[lo:hi, :], h)
            p = p_ref[base + lo : base + hi, tile]
            ratio = (p.astype(f32) * inverse(model)).astype(bf16)
            part = dot(wt[:, lo:hi], ratio)
            numer = part if numer is None else numer + part
        if first:
            numer_ref[:, tile] = numer
        else:
            new_ref[:, tile] = (h.astype(f32) * numer * inv).astype(bf16)


def place_kernel(rows, at_ref, own_ref, other_ref, out_ref, sems):
    blocks = own_ref.shape[0] // rows
    copies = []
    for n in range(2 * blocks):
        ref, m = (own_ref, n) if n < blocks else (other_ref, n - blocks)
        start = pl.multiple_of(at_ref[n] * rows, 16)
        source = ref.at[pl.ds(m * rows, rows)]
        copies.append(pltpu.make_async_copy(source, out_ref.at[pl.ds(start, rows)], sems.at[n]))
        copies[-1].start()
    for copy in copies:
        copy.wait()


VMEM = pl.BlockSpec(memory_space=pltpu.VMEM)
HBM = pl.BlockSpec(memory_space=pltpu.HBM)
SMEM = pl.BlockSpec(memory_space=pltpu.SMEM)
ANY = pl.BlockSpec(memory_space=pl.ANY)


def call(kernel, outs, scratch, flops, *args, specs=None, out_spec=None, mib=16):
    size = sum(a.size * a.dtype.itemsize for a in args)
    size += sum(o.size * o.dtype.itemsize for o in outs)
    return pl.pallas_call(
        kernel,
        out_shape=tuple(outs),
        in_specs=specs or [VMEM] * len(args),
        out_specs=tuple([out_spec or VMEM] * len(outs)),
        scratch_shapes=scratch,
        cost_estimate=pl.CostEstimate(flops=flops, bytes_accessed=size, transcendentals=0),
        compiler_params=pltpu.CompilerParams(vmem_limit_bytes=mib * 1024 * 1024),
    )(*args)


def shape(dims, dtype):
    return jax.ShapeDtypeStruct(dims, dtype)


def analyse(at, audio, halo, kernel, weights, acts):
    bins, comps = weights.shape
    frames = acts.shape[1]
    blocks = at.shape[0]
    return call(
        functools.partial(analyse_kernel, bins // blocks),
        [shape((bins, frames), bf16), shape((comps, frames), bf16), shape((bins, comps), bf16)],
        [
            pltpu.VMEM(audio.shape, bf16),
            pltpu.VMEM(kernel.shape, bf16),
            pltpu.VMEM(acts.shape, bf16),
            pltpu.VMEM((audio.shape[0] + 16, LANES), f32),
            pltpu.VMEM((frames, 2 * HOP), bf16),
            pltpu.VMEM((comps, bins), bf16),
            pltpu.SemaphoreType.DMA,
            pltpu.SemaphoreType.DMA((2 * blocks,)),
            pltpu.SemaphoreType.DMA((blocks,)),
            pltpu.SemaphoreType.DMA,
        ],
        2 * bins * frames * (4 * HOP + 2 * comps),
        at, halo, *[pltpu.with_memory_space_constraint(x, pltpu.HBM) for x in (audio, kernel, weights, acts)],
        specs=[SMEM, VMEM, HBM, HBM, HBM, HBM],
        mib=32,
    )


def template_numerator(size, power, p_base, weights, w_base, acts, extras):
    comps = acts.shape[0]
    outs = [shape((size + 16, comps), bf16) if "send" in extras else shape((size, comps), f32)]
    if "totals" in extras:
        outs.append(shape((8, comps), f32))
    if "templates" in extras:
        outs.append(shape((size, comps), bf16))
    if "copy" in extras:
        outs.append(shape(acts.shape, bf16))
    kernel = functools.partial(template_kernel, size, p_base, w_base, extras)
    return call(kernel, outs, [], 4 * size * acts.size, power, weights, acts)


def activation_numerator(power, base, weights, acts):
    size, comps = weights.shape
    return call(
        functools.partial(activation_kernel, True, base),
        [shape(acts.shape, f32), shape((comps, 128), f32)],
        [pltpu.VMEM((comps, size), bf16)],
        4 * size * acts.size, power, weights, acts,
    )


def new_activations(power, base, weights, acts, numer, colsum):
    size, comps = weights.shape
    return call(
        functools.partial(activation_kernel, False, base),
        [shape(acts.shape, bf16)],
        [pltpu.VMEM((comps, size), bf16)],
        4 * size * acts.size, power, weights, acts, numer, colsum,
    )[0]


def halo_rows(audio, peers):
    me = lax.axis_index("tm")
    odd = me % 2 == 1
    rows = HALF // LANES
    head, tail = audio[:rows], audio[audio.shape[0] - rows :]
    inner = [(i, i ^ 1) for i in range(peers)]
    outer = [(i, (i + 1) % peers if i % 2 else (i - 1) % peers) for i in range(peers)]
    one = lax.ppermute(jnp.where(odd, head, tail), "tm", inner)
    two = lax.ppermute(jnp.where(odd, tail, head), "tm", outer)
    two = jnp.where((me == 0) | (me == peers - 1), jnp.zeros_like(two), two)
    left = jnp.where(odd, one, two)
    right = jnp.where(odd, two, one)
    return jnp.concatenate([left, right], axis=0).astype(f32)


class Group:
    def __init__(self, bits, peers):
        me = lax.axis_index("tm")
        self.size = 1 << len(bits)
        self.me = sum(((me // b) % 2) << j for j, b in enumerate(bits))
        self.others = []
        for code in range(1, self.size):
            mask = sum(b for j, b in enumerate(bits) if code >> j & 1)
            self.others.append((code, [(i, i ^ mask) for i in range(peers)]))


def groups_of(peers):
    bits = [1 << b for b in range(peers.bit_length() - 1)]
    return Group(bits[:1], peers), Group(bits[1:3], peers), [Group([b], peers) for b in bits[3:]]


def halves_of(totals):
    hi = totals.astype(bf16)
    lo = (totals - hi.astype(f32)).astype(bf16)
    return (hi, lo), hi.astype(f32) + lo.astype(f32)


def swap(send, halves, perm):
    if halves is None:
        return lax.ppermute(send, "tm", perm), None
    rows = send.shape[0]
    pad = jnp.zeros((14, send.shape[1]), bf16)
    got = lax.ppermute(jnp.concatenate([send, halves[0][None], halves[1][None], pad], axis=0), "tm", perm)
    return got[:rows], got[rows].astype(f32) + got[rows + 1].astype(f32)


def sum_chips(mine, others, total, quad, pairs, direct):
    halves = None
    if total is not None:
        halves, total = halves_of(total)
    perms = [perm for _, perm in quad.others]
    if direct:
        for other, perm in zip(others, perms):
            more, part = swap(other.astype(bf16), halves, perm)
            mine = mine + more.astype(f32)
            total = None if total is None else total + part
    else:
        rows = mine.shape[0]
        more = lax.ppermute(jnp.concatenate([others[0], others[2]]).astype(bf16), "tm", perms[0])
        far = (others[1] + more[rows:].astype(f32)).astype(bf16)
        mine = mine + more[:rows].astype(f32)
        mine = mine + lax.ppermute(far, "tm", perms[1]).astype(f32)
    for group in pairs:
        if total is not None:
            halves, total = halves_of(total)
        mine = mine.astype(bf16)
        more, part = swap(mine, halves, group.others[0][1])
        mine = mine.astype(f32) + more.astype(f32)
        total = None if total is None else total + part
    return mine, total


def spread(part, quad, direct):
    perms = [perm for _, perm in quad.others]
    if direct:
        return [part] + [lax.ppermute(part, "tm", perm) for perm in perms]
    rows = part.shape[0]
    far = lax.ppermute(part, "tm", perms[1])
    got = lax.ppermute(jnp.concatenate([part, far]), "tm", perms[0])
    return [part, got[:rows], far, got[rows:]]


def on_device(audio, kernel, templates, activations):
    peers = lax.axis_size("tm")
    bins = templates.shape[0]
    size = bins // 2
    audio = audio.reshape(audio.shape[0] // LANES, LANES)
    halo = halo_rows(audio, peers)
    core, quad, pairs = groups_of(peers)
    rows = size // quad.size
    cuts = [0, (rows // 2 + 15) // 16 * 16, rows]
    order = [quad.me] + [quad.me ^ code for code, _ in quad.others]
    at = [core.me * quad.size + q for q in order] + [(1 - core.me) * quad.size + q for q in order]
    at = jnp.stack(at).astype(jnp.int32)
    power, acts, weights = analyse(at, audio, halo, kernel, templates, activations)
    own_w, other_w, base = weights, weights, size
    for step in range(ITERS):
        last = step == ITERS - 1
        (send,) = template_numerator(size, power, size, other_w, base, acts, ("send",))
        got = lax.ppermute(send, "tm", core.others[0][1])
        rest, total = template_numerator(size - rows, power, rows, own_w, rows, acts, ("totals",))
        extras = ("templates",) + (("copy",) if last else ())
        mine, weights, *copied = template_numerator(rows, power, 0, own_w, 0, acts, extras)
        rest = rest + got[rows:size].astype(f32)
        mine = mine + got[:rows].astype(f32)
        total = total[0] + (got[size].astype(f32) + got[size + 1].astype(f32))
        pieces, rowsum = [], None
        for lo, hi in zip(cuts[:-1], cuts[1:]):
            others = [rest[n * rows + lo : n * rows + hi] for n in range(quad.size - 1)]
            part, tot = sum_chips(
                mine[lo:hi], others, total if lo == 0 else None, quad, pairs, DIRECT[0][lo == 0]
            )
            rowsum = tot if lo == 0 else rowsum
            part = (weights[lo:hi].astype(f32) * part / rowsum[None, :]).astype(bf16)
            pieces.append(spread(part, quad, DIRECT[1][lo == 0]))
        own_w = jnp.concatenate([piece[n] for n in range(quad.size) for piece in pieces], axis=0)
        other_w, base = lax.ppermute(own_w, "tm", core.others[0][1]), 0
        if not last:
            numer, colsum = activation_numerator(power, 0, own_w, acts)
            acts = new_activations(power, size, other_w, acts, numer, colsum)
    kernel = functools.partial(place_kernel, rows)
    out = call(
        kernel, [shape(templates.shape, bf16)], [pltpu.SemaphoreType.DMA((at.shape[0],))], 0,
        at, own_w, other_w, specs=[SMEM, ANY, ANY], out_spec=ANY,
    )
    return (copied[0], out[0])


def solution(mesh):
    in_specs = (P(("groups", "tm")), P(), P(), P(None, ("groups", "tm")))
    out_specs = (P(None, ("groups", "tm")), P("groups", None))
    return jax.shard_map(
        on_device, mesh=mesh, in_specs=in_specs, out_specs=out_specs, check_vma=False
    )
```

```python
import functools

import jax
import jax.numpy as jnp
from jax import lax
from jax.experimental import pallas as pl
from jax.experimental.pallas import tpu as pltpu
from jax.sharding import PartitionSpec as P

HOP = 512
ITERS = 2
HALF = 256
TILE = 256
SPAN = 1024
LANES = 128
bf16 = jnp.bfloat16
f32 = jnp.float32
DIRECT = ((False, True), (True, False))
NT = (((1,), (1,)), ((), ()))


def inverse(x):
    r = pl.reciprocal(x, approx=True)
    return r * (2.0 - x * r)


def dot(a, b):
    return jnp.dot(a, b, preferred_element_type=f32)


def dot_nt(a, b):
    return lax.dot_general(a, b, NT, preferred_element_type=f32)


def row_blocks(rows):
    if rows < TILE:
        return [(0, rows)]
    first = rows % TILE
    cuts = [0] + list(range(first + TILE if first else TILE, rows + 1, TILE))
    return list(zip(cuts[:-1], cuts[1:]))


def analyse_kernel(rows, at_ref, halo_ref, a_hbm, k_hbm, w_hbm, h_hbm, p_ref, new_ref, w_ref,
                   a_ref, k_ref, h_ref, wide, frame, wt, a_sem, k_sem, w_sem, h_sem):
    bins = w_ref.shape[0]
    frames = h_ref.shape[1]
    blocks = row_blocks(bins)
    a_copy = pltpu.make_async_copy(a_hbm, a_ref, a_sem)
    a_copy.start()
    k_copies, w_copies = [], []
    for n in range(bins // rows):
        start = pl.multiple_of(at_ref[n] * rows, 16)
        here = pl.ds(n * rows, rows)
        for m in range(2):
            k_copies.append(
                pltpu.make_async_copy(
                    k_hbm.at[pl.ds(m * bins + start, rows)],
                    k_ref.at[pl.ds(m * bins + n * rows, rows)],
                    k_sem.at[2 * n + m],
                )
            )
        w_copies.append(pltpu.make_async_copy(w_hbm.at[pl.ds(start, rows)], w_ref.at[here], w_sem.at[n]))
    h_copy = pltpu.make_async_copy(h_hbm, h_ref, h_sem)
    for copy in k_copies + w_copies + [h_copy]:
        copy.start()

    a_copy.wait()
    wide[8 : 8 + a_ref.shape[0], :] = a_ref[...].astype(f32)
    wide[6:8, :] = halo_ref[0:2, :]
    wide[8 + a_ref.shape[0] : 10 + a_ref.shape[0], :] = halo_ref[2:4, :]
    for j in range(2 * HOP // LANES):
        strip = wide[pl.ds(6 + j, frames, stride=HOP // LANES), :]
        frame[:, j * LANES : (j + 1) * LANES] = strip.astype(bf16)

    waited = 0
    for lo, hi in blocks:
        while waited < -(-hi // rows):
            k_copies[2 * waited].wait()
            k_copies[2 * waited + 1].wait()
            waited += 1
        for t in range(0, frames, 512):
            f = frame[t : t + 512, :]
            re = dot_nt(k_ref[lo:hi, :], f)
            im = dot_nt(k_ref[bins + lo : bins + hi, :], f)
            p_ref[lo:hi, t : t + 512] = (re * re + im * im).astype(bf16)

    for copy in w_copies + [h_copy]:
        copy.wait()
    wt[...] = w_ref[...].T
    inv = inverse(jnp.sum(wt[...].astype(f32), axis=1, keepdims=True))
    for t in range(0, frames, TILE):
        tile = slice(t, t + TILE)
        h = h_ref[:, tile]
        numer = None
        for lo, hi in blocks:
            model = dot(w_ref[lo:hi, :], h)
            ratio = (p_ref[lo:hi, tile].astype(f32) * inverse(model)).astype(bf16)
            part = dot(wt[:, lo:hi], ratio)
            numer = part if numer is None else numer + part
        new_ref[:, tile] = (h.astype(f32) * numer * inv).astype(bf16)


def template_kernel(size, p_base, w_base, extras, p_ref, w_ref, h_ref, *outs):
    frames = h_ref.shape[1]
    outs = list(outs)
    numw_ref = outs.pop(0)
    for lo, hi in row_blocks(size):
        w = w_ref[w_base + lo : w_base + hi, :]
        acc = None
        for t in range(0, frames, SPAN):
            h = h_ref[:, t : t + SPAN]
            model = dot(w, h)
            p = p_ref[p_base + lo : p_base + hi, t : t + SPAN]
            ratio = (p.astype(f32) * inverse(model)).astype(bf16)
            part = dot_nt(ratio, h)
            acc = part if acc is None else acc + part
        numw_ref[lo:hi, :] = acc.astype(numw_ref.dtype)
    if "send" in extras or "totals" in extras:
        total = dot_nt(jnp.ones((16, frames), bf16), h_ref[...])
        high = total.astype(bf16).astype(f32)
        low = (total - high).astype(bf16).astype(f32)
        if "send" in extras:
            row = lax.broadcasted_iota(jnp.int32, total.shape, 0)
            both = jnp.where(row == 0, high, jnp.where(row == 1, low, 0.0))
            numw_ref[size : size + 16, :] = both.astype(bf16)
        else:
            outs.pop(0)[...] = (high + low)[:8]
    if "templates" in extras:
        outs.pop(0)[...] = w_ref[w_base : w_base + size, :]


def activation_kernel(first, base, p_ref, w_ref, h_ref, *refs):
    if first:
        numer_ref, col_ref, wt = refs
    else:
        old_ref, oldcol_ref, new_ref, wt = refs
    frames = h_ref.shape[1]
    wt[...] = w_ref[...].T
    col = jnp.sum(wt[...].astype(f32), axis=1, keepdims=True)
    if first:
        col_ref[...] = jnp.broadcast_to(col, col_ref.shape)
    else:
        inv = inverse(col + oldcol_ref[:, :1])
    for t in range(0, frames, TILE):
        tile = slice(t, t + TILE)
        h = h_ref[:, tile]
        numer = None if first else old_ref[:, tile]
        for lo, hi in row_blocks(w_ref.shape[0]):
            model = dot(w_ref[lo:hi, :], h)
            p = p_ref[base + lo : base + hi, tile]
            ratio = (p.astype(f32) * inverse(model)).astype(bf16)
            part = dot(wt[:, lo:hi], ratio)
            numer = part if numer is None else numer + part
        if first:
            numer_ref[:, tile] = numer
        else:
            new_ref[:, tile] = (h.astype(f32) * numer * inv).astype(bf16)


def place_kernel(rows, at_ref, own_ref, acts_ref, out_ref, acts_out_ref, sems):
    copies = [pltpu.make_async_copy(acts_ref, acts_out_ref, sems.at[at_ref.shape[0]])]
    copies[0].start()
    for n in range(at_ref.shape[0]):
        start = pl.multiple_of(at_ref[n] * rows, 16)
        source = own_ref.at[pl.ds(n * rows, rows)]
        copies.append(pltpu.make_async_copy(source, out_ref.at[pl.ds(start, rows)], sems.at[n]))
        copies[-1].start()
    for copy in copies:
        copy.wait()


def place_other_kernel(rows, at_ref, other_ref, half_ref, out_ref, sems):
    copies = []
    for n in range(at_ref.shape[0]):
        start = pl.multiple_of(at_ref[n] * rows, 16)
        source = other_ref.at[pl.ds(n * rows, rows)]
        copies.append(pltpu.make_async_copy(source, out_ref.at[pl.ds(start, rows)], sems.at[n]))
        copies[-1].start()
    for copy in copies:
        copy.wait()


VMEM = pl.BlockSpec(memory_space=pltpu.VMEM)
HBM = pl.BlockSpec(memory_space=pltpu.HBM)
SMEM = pl.BlockSpec(memory_space=pltpu.SMEM)
ANY = pl.BlockSpec(memory_space=pl.ANY)


def call(kernel, outs, scratch, flops, *args, specs=None, out_spec=None, aliases={}, mib=16):
    size = sum(a.size * a.dtype.itemsize for a in args)
    size += sum(o.size * o.dtype.itemsize for o in outs)
    return pl.pallas_call(
        kernel,
        out_shape=tuple(outs),
        in_specs=specs or [VMEM] * len(args),
        out_specs=tuple([out_spec or VMEM] * len(outs)),
        scratch_shapes=scratch,
        input_output_aliases=aliases,
        cost_estimate=pl.CostEstimate(flops=flops, bytes_accessed=size, transcendentals=0),
        compiler_params=pltpu.CompilerParams(vmem_limit_bytes=mib * 1024 * 1024),
    )(*args)


def shape(dims, dtype):
    return jax.ShapeDtypeStruct(dims, dtype)


def analyse(at, audio, halo, kernel, weights, acts):
    bins, comps = weights.shape
    frames = acts.shape[1]
    blocks = at.shape[0]
    return call(
        functools.partial(analyse_kernel, bins // blocks),
        [shape((bins, frames), bf16), shape((comps, frames), bf16), shape((bins, comps), bf16)],
        [
            pltpu.VMEM(audio.shape, bf16),
            pltpu.VMEM(kernel.shape, bf16),
            pltpu.VMEM(acts.shape, bf16),
            pltpu.VMEM((audio.shape[0] + 16, LANES), f32),
            pltpu.VMEM((frames, 2 * HOP), bf16),
            pltpu.VMEM((comps, bins), bf16),
            pltpu.SemaphoreType.DMA,
            pltpu.SemaphoreType.DMA((2 * blocks,)),
            pltpu.SemaphoreType.DMA((blocks,)),
            pltpu.SemaphoreType.DMA,
        ],
        2 * bins * frames * (4 * HOP + 2 * comps),
        at, halo, *[pltpu.with_memory_space_constraint(x, pltpu.HBM) for x in (audio, kernel, weights, acts)],
        specs=[SMEM, VMEM, HBM, HBM, HBM, HBM],
        mib=32,
    )


def template_numerator(size, power, p_base, weights, w_base, acts, extras):
    comps = acts.shape[0]
    outs = [shape((size + 16, comps), bf16) if "send" in extras else shape((size, comps), f32)]
    if "totals" in extras:
        outs.append(shape((8, comps), f32))
    if "templates" in extras:
        outs.append(shape((size, comps), bf16))
    kernel = functools.partial(template_kernel, size, p_base, w_base, extras)
    return call(kernel, outs, [], 4 * size * acts.size, power, weights, acts)


def activation_numerator(power, base, weights, acts):
    size, comps = weights.shape
    return call(
        functools.partial(activation_kernel, True, base),
        [shape(acts.shape, f32), shape((comps, 128), f32)],
        [pltpu.VMEM((comps, size), bf16)],
        4 * size * acts.size, power, weights, acts,
    )


def new_activations(power, base, weights, acts, numer, colsum):
    size, comps = weights.shape
    return call(
        functools.partial(activation_kernel, False, base),
        [shape(acts.shape, bf16)],
        [pltpu.VMEM((comps, size), bf16)],
        4 * size * acts.size, power, weights, acts, numer, colsum,
    )[0]


def halo_rows(audio, peers):
    me = lax.axis_index("tm")
    odd = me % 2 == 1
    rows = HALF // LANES
    head, tail = audio[:rows], audio[audio.shape[0] - rows :]
    inner = [(i, i ^ 1) for i in range(peers)]
    outer = [(i, (i + 1) % peers if i % 2 else (i - 1) % peers) for i in range(peers)]
    one = lax.ppermute(jnp.where(odd, head, tail), "tm", inner)
    two = lax.ppermute(jnp.where(odd, tail, head), "tm", outer)
    two = jnp.where((me == 0) | (me == peers - 1), jnp.zeros_like(two), two)
    left = jnp.where(odd, one, two)
    right = jnp.where(odd, two, one)
    return jnp.concatenate([left, right], axis=0).astype(f32)


class Group:
    def __init__(self, bits, peers):
        me = lax.axis_index("tm")
        self.size = 1 << len(bits)
        self.me = sum(((me // b) % 2) << j for j, b in enumerate(bits))
        self.others = []
        for code in range(1, self.size):
            mask = sum(b for j, b in enumerate(bits) if code >> j & 1)
            self.others.append((code, [(i, i ^ mask) for i in range(peers)]))


def groups_of(peers):
    bits = [1 << b for b in range(peers.bit_length() - 1)]
    return Group(bits[:1], peers), Group(bits[1:3], peers), [Group([b], peers) for b in bits[3:]]


def halves_of(totals):
    hi = totals.astype(bf16)
    lo = (totals - hi.astype(f32)).astype(bf16)
    return (hi, lo), hi.astype(f32) + lo.astype(f32)


def swap(send, halves, perm):
    if halves is None:
        return lax.ppermute(send, "tm", perm), None
    rows = send.shape[0]
    pad = jnp.zeros((14, send.shape[1]), bf16)
    got = lax.ppermute(jnp.concatenate([send, halves[0][None], halves[1][None], pad], axis=0), "tm", perm)
    return got[:rows], got[rows].astype(f32) + got[rows + 1].astype(f32)


def sum_chips(mine, others, total, quad, pairs, direct):
    halves = None
    if total is not None:
        halves, total = halves_of(total)
    perms = [perm for _, perm in quad.others]
    if direct:
        for other, perm in zip(others, perms):
            more, part = swap(other.astype(bf16), halves, perm)
            mine = mine + more.astype(f32)
            total = None if total is None else total + part
    else:
        rows = mine.shape[0]
        more = lax.ppermute(jnp.concatenate([others[0], others[2]]).astype(bf16), "tm", perms[0])
        far = (others[1] + more[rows:].astype(f32)).astype(bf16)
        mine = mine + more[:rows].astype(f32)
        mine = mine + lax.ppermute(far, "tm", perms[1]).astype(f32)
    for group in pairs:
        if total is not None:
            halves, total = halves_of(total)
        mine = mine.astype(bf16)
        more, part = swap(mine, halves, group.others[0][1])
        mine = mine.astype(f32) + more.astype(f32)
        total = None if total is None else total + part
    return mine, total


def spread(part, quad, direct):
    perms = [perm for _, perm in quad.others]
    if direct:
        return [part] + [lax.ppermute(part, "tm", perm) for perm in perms]
    rows = part.shape[0]
    far = lax.ppermute(part, "tm", perms[1])
    got = lax.ppermute(jnp.concatenate([part, far]), "tm", perms[0])
    return [part, got[:rows], far, got[rows:]]


def on_device(audio, kernel, templates, activations):
    peers = lax.axis_size("tm")
    bins = templates.shape[0]
    size = bins // 2
    audio = audio.reshape(audio.shape[0] // LANES, LANES)
    halo = halo_rows(audio, peers)
    core, quad, pairs = groups_of(peers)
    rows = size // quad.size
    cuts = [0, (rows // 2 + 15) // 16 * 16, rows]
    order = [quad.me] + [quad.me ^ code for code, _ in quad.others]
    at = [core.me * quad.size + q for q in order] + [(1 - core.me) * quad.size + q for q in order]
    at = jnp.stack(at).astype(jnp.int32)
    power, acts, weights = analyse(at, audio, halo, kernel, templates, activations)
    own_w, other_w, base = weights, weights, size
    for step in range(ITERS):
        last = step == ITERS - 1
        (send,) = template_numerator(size, power, size, other_w, base, acts, ("send",))
        got = lax.ppermute(send, "tm", core.others[0][1])
        rest, total = template_numerator(size - rows, power, rows, own_w, rows, acts, ("totals",))
        mine, weights = template_numerator(rows, power, 0, own_w, 0, acts, ("templates",))
        rest = rest + got[rows:size].astype(f32)
        mine = mine + got[:rows].astype(f32)
        total = total[0] + (got[size].astype(f32) + got[size + 1].astype(f32))
        pieces, rowsum = [], None
        for lo, hi in zip(cuts[:-1], cuts[1:]):
            others = [rest[n * rows + lo : n * rows + hi] for n in range(quad.size - 1)]
            part, tot = sum_chips(
                mine[lo:hi], others, total if lo == 0 else None, quad, pairs, DIRECT[0][lo == 0]
            )
            rowsum = tot if lo == 0 else rowsum
            part = (weights[lo:hi].astype(f32) * part / rowsum[None, :]).astype(bf16)
            pieces.append(spread(part, quad, DIRECT[1][lo == 0]))
        own_w = jnp.concatenate([piece[n] for n in range(quad.size) for piece in pieces], axis=0)
        other_w, base = lax.ppermute(own_w, "tm", core.others[0][1]), 0
        if not last:
            numer, colsum = activation_numerator(power, 0, own_w, acts)
            acts = new_activations(power, size, other_w, acts, numer, colsum)
    out, acts = call(
        functools.partial(place_kernel, rows),
        [shape(templates.shape, bf16), shape(acts.shape, bf16)],
        [pltpu.SemaphoreType.DMA((quad.size + 1,))],
        2 * acts.size * acts.shape[0],
        at[: quad.size], own_w, acts, specs=[SMEM, ANY, ANY], out_spec=ANY,
    )
    (out,) = call(
        functools.partial(place_other_kernel, rows),
        [shape(templates.shape, bf16)],
        [pltpu.SemaphoreType.DMA((quad.size,))],
        0,
        at[quad.size :], other_w, out, specs=[SMEM, ANY, ANY], out_spec=ANY, aliases={2: 0},
    )
    return (acts, out)


def solution(mesh):
    in_specs = (P(("groups", "tm")), P(), P(), P(None, ("groups", "tm")))
    out_specs = (P(None, ("groups", "tm")), P("groups", None))
    return jax.shard_map(
        on_device, mesh=mesh, in_specs=in_specs, out_specs=out_specs, check_vma=False
    )
```

```python
import functools

import jax
import jax.numpy as jnp
from jax import lax
from jax.experimental import pallas as pl
from jax.experimental.pallas import tpu as pltpu
from jax.sharding import PartitionSpec as P

HOP = 512
ITERS = 2
HALF = 256
TILE = 256
SPAN = 1024
LANES = 128
bf16 = jnp.bfloat16
f32 = jnp.float32
DIRECT = ((False, True), (True, False))
NT = (((1,), (1,)), ((), ()))


def inverse(x):
    r = pl.reciprocal(x, approx=True)
    return r * (2.0 - x * r)


def dot(a, b):
    return jnp.dot(a, b, preferred_element_type=f32)


def dot_nt(a, b):
    return lax.dot_general(a, b, NT, preferred_element_type=f32)


def row_blocks(rows):
    if rows < TILE:
        return [(0, rows)]
    first = rows % TILE
    cuts = [0] + list(range(first + TILE if first else TILE, rows + 1, TILE))
    return list(zip(cuts[:-1], cuts[1:]))


def analyse_kernel(rows, at_ref, halo_ref, a_hbm, k_hbm, w_hbm, h_hbm, p_ref, new_ref, w_ref,
                   a_ref, k_ref, h_ref, wide, frame, wt, a_sem, k_sem, w_sem, h_sem):
    bins = w_ref.shape[0]
    frames = h_ref.shape[1]
    blocks = row_blocks(bins)
    a_copy = pltpu.make_async_copy(a_hbm, a_ref, a_sem)
    a_copy.start()
    k_copies, w_copies = [], []
    for n in range(bins // rows):
        start = pl.multiple_of(at_ref[n] * rows, 16)
        here = pl.ds(n * rows, rows)
        for m in range(2):
            k_copies.append(
                pltpu.make_async_copy(
                    k_hbm.at[pl.ds(m * bins + start, rows)],
                    k_ref.at[pl.ds(m * bins + n * rows, rows)],
                    k_sem.at[2 * n + m],
                )
            )
        w_copies.append(pltpu.make_async_copy(w_hbm.at[pl.ds(start, rows)], w_ref.at[here], w_sem.at[n]))
    h_copy = pltpu.make_async_copy(h_hbm, h_ref, h_sem)
    for copy in k_copies + w_copies + [h_copy]:
        copy.start()

    a_copy.wait()
    wide[8 : 8 + a_ref.shape[0], :] = a_ref[...].astype(f32)
    wide[6:8, :] = halo_ref[0:2, :]
    wide[8 + a_ref.shape[0] : 10 + a_ref.shape[0], :] = halo_ref[2:4, :]
    stride = HOP // LANES

    def build(t):
        for j in range(2 * HOP // LANES):
            strip = wide[pl.ds(6 + j + t * stride, 512, stride=stride), :]
            frame[t : t + 512, j * LANES : (j + 1) * LANES] = strip.astype(bf16)

    build(0)
    waited = 0
    for lo, hi in blocks:
        while waited < -(-hi // rows):
            k_copies[2 * waited].wait()
            k_copies[2 * waited + 1].wait()
            waited += 1
        for t in range(0, frames, 512):
            if lo == 0 and t + 512 < frames:
                build(t + 512)
            f = frame[t : t + 512, :]
            re = dot_nt(k_ref[lo:hi, :], f)
            im = dot_nt(k_ref[bins + lo : bins + hi, :], f)
            p_ref[lo:hi, t : t + 512] = (re * re + im * im).astype(bf16)

    for copy in w_copies + [h_copy]:
        copy.wait()
    wt[...] = w_ref[...].T
    inv = inverse(jnp.sum(wt[...].astype(f32), axis=1, keepdims=True))
    for t in range(0, frames, TILE):
        tile = slice(t, t + TILE)
        h = h_ref[:, tile]
        numer = None
        for lo, hi in blocks:
            model = dot(w_ref[lo:hi, :], h)
            ratio = (p_ref[lo:hi, tile].astype(f32) * inverse(model)).astype(bf16)
            part = dot(wt[:, lo:hi], ratio)
            numer = part if numer is None else numer + part
        new_ref[:, tile] = (h.astype(f32) * numer * inv).astype(bf16)


def template_kernel(size, p_base, w_base, extras, p_ref, w_ref, h_ref, *outs):
    frames = h_ref.shape[1]
    outs = list(outs)
    numw_ref = outs.pop(0)
    for lo, hi in row_blocks(size):
        w = w_ref[w_base + lo : w_base + hi, :]
        acc = None
        for t in range(0, frames, SPAN):
            h = h_ref[:, t : t + SPAN]
            model = dot(w, h)
            p = p_ref[p_base + lo : p_base + hi, t : t + SPAN]
            ratio = (p.astype(f32) * inverse(model)).astype(bf16)
            part = dot_nt(ratio, h)
            acc = part if acc is None else acc + part
        numw_ref[lo:hi, :] = acc.astype(numw_ref.dtype)
    if "send" in extras or "totals" in extras:
        total = dot_nt(jnp.ones((16, frames), bf16), h_ref[...])
        high = total.astype(bf16).astype(f32)
        low = (total - high).astype(bf16).astype(f32)
        if "send" in extras:
            row = lax.broadcasted_iota(jnp.int32, total.shape, 0)
            both = jnp.where(row == 0, high, jnp.where(row == 1, low, 0.0))
            numw_ref[size : size + 16, :] = both.astype(bf16)
        else:
            outs.pop(0)[...] = (high + low)[:8]
    if "templates" in extras:
        outs.pop(0)[...] = w_ref[w_base : w_base + size, :]


def activation_kernel(first, base, p_ref, w_ref, h_ref, *refs):
    if first:
        numer_ref, col_ref, wt = refs
    else:
        old_ref, oldcol_ref, new_ref, wt = refs
    frames = h_ref.shape[1]
    wt[...] = w_ref[...].T
    col = jnp.sum(wt[...].astype(f32), axis=1, keepdims=True)
    if first:
        col_ref[...] = jnp.broadcast_to(col, col_ref.shape)
    else:
        inv = inverse(col + oldcol_ref[:, :1])
    for t in range(0, frames, TILE):
        tile = slice(t, t + TILE)
        h = h_ref[:, tile]
        numer = None if first else old_ref[:, tile]
        for lo, hi in row_blocks(w_ref.shape[0]):
            model = dot(w_ref[lo:hi, :], h)
            p = p_ref[base + lo : base + hi, tile]
            ratio = (p.astype(f32) * inverse(model)).astype(bf16)
            part = dot(wt[:, lo:hi], ratio)
            numer = part if numer is None else numer + part
        if first:
            numer_ref[:, tile] = numer
        else:
            new_ref[:, tile] = (h.astype(f32) * numer * inv).astype(bf16)


def place_kernel(rows, at_ref, own_ref, acts_ref, out_ref, acts_out_ref, sems):
    copies = [pltpu.make_async_copy(acts_ref, acts_out_ref, sems.at[at_ref.shape[0]])]
    copies[0].start()
    for n in range(at_ref.shape[0]):
        start = pl.multiple_of(at_ref[n] * rows, 16)
        source = own_ref.at[pl.ds(n * rows, rows)]
        copies.append(pltpu.make_async_copy(source, out_ref.at[pl.ds(start, rows)], sems.at[n]))
        copies[-1].start()
    for copy in copies:
        copy.wait()


def place_other_kernel(rows, at_ref, other_ref, half_ref, out_ref, sems):
    copies = []
    for n in range(at_ref.shape[0]):
        start = pl.multiple_of(at_ref[n] * rows, 16)
        source = other_ref.at[pl.ds(n * rows, rows)]
        copies.append(pltpu.make_async_copy(source, out_ref.at[pl.ds(start, rows)], sems.at[n]))
        copies[-1].start()
    for copy in copies:
        copy.wait()


VMEM = pl.BlockSpec(memory_space=pltpu.VMEM)
HBM = pl.BlockSpec(memory_space=pltpu.HBM)
SMEM = pl.BlockSpec(memory_space=pltpu.SMEM)
ANY = pl.BlockSpec(memory_space=pl.ANY)


def call(kernel, outs, scratch, flops, *args, specs=None, out_spec=None, aliases={}, mib=16):
    size = sum(a.size * a.dtype.itemsize for a in args)
    size += sum(o.size * o.dtype.itemsize for o in outs)
    return pl.pallas_call(
        kernel,
        out_shape=tuple(outs),
        in_specs=specs or [VMEM] * len(args),
        out_specs=tuple([out_spec or VMEM] * len(outs)),
        scratch_shapes=scratch,
        input_output_aliases=aliases,
        cost_estimate=pl.CostEstimate(flops=flops, bytes_accessed=size, transcendentals=0),
        compiler_params=pltpu.CompilerParams(vmem_limit_bytes=mib * 1024 * 1024),
    )(*args)


def shape(dims, dtype):
    return jax.ShapeDtypeStruct(dims, dtype)


def analyse(at, audio, halo, kernel, weights, acts):
    bins, comps = weights.shape
    frames = acts.shape[1]
    blocks = at.shape[0]
    return call(
        functools.partial(analyse_kernel, bins // blocks),
        [shape((bins, frames), bf16), shape((comps, frames), bf16), shape((bins, comps), bf16)],
        [
            pltpu.VMEM(audio.shape, bf16),
            pltpu.VMEM(kernel.shape, bf16),
            pltpu.VMEM(acts.shape, bf16),
            pltpu.VMEM((audio.shape[0] + 16, LANES), f32),
            pltpu.VMEM((frames, 2 * HOP), bf16),
            pltpu.VMEM((comps, bins), bf16),
            pltpu.SemaphoreType.DMA,
            pltpu.SemaphoreType.DMA((2 * blocks,)),
            pltpu.SemaphoreType.DMA((blocks,)),
            pltpu.SemaphoreType.DMA,
        ],
        2 * bins * frames * (4 * HOP + 2 * comps),
        at, halo, *[pltpu.with_memory_space_constraint(x, pltpu.HBM) for x in (audio, kernel, weights, acts)],
        specs=[SMEM, VMEM, HBM, HBM, HBM, HBM],
        mib=32,
    )


def template_numerator(size, power, p_base, weights, w_base, acts, extras):
    comps = acts.shape[0]
    outs = [shape((size + 16, comps), bf16) if "send" in extras else shape((size, comps), f32)]
    if "totals" in extras:
        outs.append(shape((8, comps), f32))
    if "templates" in extras:
        outs.append(shape((size, comps), bf16))
    kernel = functools.partial(template_kernel, size, p_base, w_base, extras)
    return call(kernel, outs, [], 4 * size * acts.size, power, weights, acts)


def activation_numerator(power, base, weights, acts):
    size, comps = weights.shape
    return call(
        functools.partial(activation_kernel, True, base),
        [shape(acts.shape, f32), shape((comps, 128), f32)],
        [pltpu.VMEM((comps, size), bf16)],
        4 * size * acts.size, power, weights, acts,
    )


def new_activations(power, base, weights, acts, numer, colsum):
    size, comps = weights.shape
    return call(
        functools.partial(activation_kernel, False, base),
        [shape(acts.shape, bf16)],
        [pltpu.VMEM((comps, size), bf16)],
        4 * size * acts.size, power, weights, acts, numer, colsum,
    )[0]


def halo_rows(audio, peers):
    me = lax.axis_index("tm")
    odd = me % 2 == 1
    rows = HALF // LANES
    head, tail = audio[:rows], audio[audio.shape[0] - rows :]
    inner = [(i, i ^ 1) for i in range(peers)]
    outer = [(i, (i + 1) % peers if i % 2 else (i - 1) % peers) for i in range(peers)]
    one = lax.ppermute(jnp.where(odd, head, tail), "tm", inner)
    two = lax.ppermute(jnp.where(odd, tail, head), "tm", outer)
    two = jnp.where((me == 0) | (me == peers - 1), jnp.zeros_like(two), two)
    left = jnp.where(odd, one, two)
    right = jnp.where(odd, two, one)
    return jnp.concatenate([left, right], axis=0).astype(f32)


class Group:
    def __init__(self, bits, peers):
        me = lax.axis_index("tm")
        self.size = 1 << len(bits)
        self.me = sum(((me // b) % 2) << j for j, b in enumerate(bits))
        self.others = []
        for code in range(1, self.size):
            mask = sum(b for j, b in enumerate(bits) if code >> j & 1)
            self.others.append((code, [(i, i ^ mask) for i in range(peers)]))


def groups_of(peers):
    bits = [1 << b for b in range(peers.bit_length() - 1)]
    return Group(bits[:1], peers), Group(bits[1:3], peers), [Group([b], peers) for b in bits[3:]]


def halves_of(totals):
    hi = totals.astype(bf16)
    lo = (totals - hi.astype(f32)).astype(bf16)
    return (hi, lo), hi.astype(f32) + lo.astype(f32)


def swap(send, halves, perm):
    if halves is None:
        return lax.ppermute(send, "tm", perm), None
    rows = send.shape[0]
    pad = jnp.zeros((14, send.shape[1]), bf16)
    got = lax.ppermute(jnp.concatenate([send, halves[0][None], halves[1][None], pad], axis=0), "tm", perm)
    return got[:rows], got[rows].astype(f32) + got[rows + 1].astype(f32)


def sum_chips(mine, others, total, quad, pairs, direct):
    halves = None
    if total is not None:
        halves, total = halves_of(total)
    perms = [perm for _, perm in quad.others]
    if direct:
        for other, perm in zip(others, perms):
            more, part = swap(other.astype(bf16), halves, perm)
            mine = mine + more.astype(f32)
            total = None if total is None else total + part
    else:
        rows = mine.shape[0]
        more = lax.ppermute(jnp.concatenate([others[0], others[2]]).astype(bf16), "tm", perms[0])
        far = (others[1] + more[rows:].astype(f32)).astype(bf16)
        mine = mine + more[:rows].astype(f32)
        mine = mine + lax.ppermute(far, "tm", perms[1]).astype(f32)
    for group in pairs:
        if total is not None:
            halves, total = halves_of(total)
        mine = mine.astype(bf16)
        more, part = swap(mine, halves, group.others[0][1])
        mine = mine.astype(f32) + more.astype(f32)
        total = None if total is None else total + part
    return mine, total


def spread(part, quad, direct):
    perms = [perm for _, perm in quad.others]
    if direct:
        return [part] + [lax.ppermute(part, "tm", perm) for perm in perms]
    rows = part.shape[0]
    far = lax.ppermute(part, "tm", perms[1])
    got = lax.ppermute(jnp.concatenate([part, far]), "tm", perms[0])
    return [part, got[:rows], far, got[rows:]]


def on_device(audio, kernel, templates, activations):
    peers = lax.axis_size("tm")
    bins = templates.shape[0]
    size = bins // 2
    audio = audio.reshape(audio.shape[0] // LANES, LANES)
    halo = halo_rows(audio, peers)
    core, quad, pairs = groups_of(peers)
    rows = size // quad.size
    cuts = [0, rows // 2 // 16 * 16, rows]
    order = [quad.me] + [quad.me ^ code for code, _ in quad.others]
    at = [core.me * quad.size + q for q in order] + [(1 - core.me) * quad.size + q for q in order]
    at = jnp.stack(at).astype(jnp.int32)
    power, acts, weights = analyse(at, audio, halo, kernel, templates, activations)
    own_w, other_w, base = weights, weights, size
    for step in range(ITERS):
        last = step == ITERS - 1
        (send,) = template_numerator(size, power, size, other_w, base, acts, ("send",))
        got = lax.ppermute(send, "tm", core.others[0][1])
        rest, total = template_numerator(size - rows, power, rows, own_w, rows, acts, ("totals",))
        mine, weights = template_numerator(rows, power, 0, own_w, 0, acts, ("templates",))
        rest = rest + got[rows:size].astype(f32)
        mine = mine + got[:rows].astype(f32)
        total = total[0] + (got[size].astype(f32) + got[size + 1].astype(f32))
        pieces, rowsum = [], None
        for lo, hi in zip(cuts[:-1], cuts[1:]):
            others = [rest[n * rows + lo : n * rows + hi] for n in range(quad.size - 1)]
            part, tot = sum_chips(
                mine[lo:hi], others, total if lo == 0 else None, quad, pairs, DIRECT[0][lo == 0]
            )
            rowsum = tot if lo == 0 else rowsum
            part = (weights[lo:hi].astype(f32) * part / rowsum[None, :]).astype(bf16)
            pieces.append(spread(part, quad, DIRECT[1][lo == 0]))
        own_w = jnp.concatenate([piece[n] for n in range(quad.size) for piece in pieces], axis=0)
        other_w, base = lax.ppermute(own_w, "tm", core.others[0][1]), 0
        if not last:
            numer, colsum = activation_numerator(power, 0, own_w, acts)
            acts = new_activations(power, size, other_w, acts, numer, colsum)
    out, acts = call(
        functools.partial(place_kernel, rows),
        [shape(templates.shape, bf16), shape(acts.shape, bf16)],
        [pltpu.SemaphoreType.DMA((quad.size + 1,))],
        2 * acts.size * acts.shape[0],
        at[: quad.size], own_w, acts, specs=[SMEM, ANY, ANY], out_spec=ANY,
    )
    (out,) = call(
        functools.partial(place_other_kernel, rows),
        [shape(templates.shape, bf16)],
        [pltpu.SemaphoreType.DMA((quad.size,))],
        0,
        at[quad.size :], other_w, out, specs=[SMEM, ANY, ANY], out_spec=ANY, aliases={2: 0},
    )
    return (acts, out)


def solution(mesh):
    in_specs = (P(("groups", "tm")), P(), P(), P(None, ("groups", "tm")))
    out_specs = (P(None, ("groups", "tm")), P("groups", None))
    return jax.shard_map(
        on_device, mesh=mesh, in_specs=in_specs, out_specs=out_specs, check_vma=False
    )
```

```python
import functools

import jax
import jax.numpy as jnp
from jax import lax
from jax.experimental import pallas as pl
from jax.experimental.pallas import tpu as pltpu
from jax.sharding import PartitionSpec as P

HOP = 512
ITERS = 2
HALF = 256
TILE = 256
SPAN = 1024
LANES = 128
bf16 = jnp.bfloat16
f32 = jnp.float32
DIRECT = ((False, True), (True, False))
NT = (((1,), (1,)), ((), ()))


def inverse(x):
    r = pl.reciprocal(x, approx=True)
    return r * (2.0 - x * r)


def dot(a, b):
    return jnp.dot(a, b, preferred_element_type=f32)


def dot_nt(a, b):
    return lax.dot_general(a, b, NT, preferred_element_type=f32)


def row_blocks(rows):
    cuts = list(range(0, max(rows - TILE, 0) + 1, TILE))
    return list(zip(cuts, cuts[1:] + [rows]))


def analyse_kernel(rows, at_ref, halo_ref, a_hbm, k_hbm, w_hbm, h_hbm, p_ref, new_ref, w_ref,
                   a_ref, k_ref, h_ref, wide, frame, wt, a_sem, k_sem, w_sem, h_sem):
    bins = w_ref.shape[0]
    frames = h_ref.shape[1]
    blocks = row_blocks(bins)
    a_copy = pltpu.make_async_copy(a_hbm, a_ref, a_sem)
    a_copy.start()
    k_copies, w_copies = [], []
    for n in range(bins // rows):
        start = pl.multiple_of(at_ref[n] * rows, 16)
        here = pl.ds(n * rows, rows)
        for m in range(2):
            k_copies.append(
                pltpu.make_async_copy(
                    k_hbm.at[pl.ds(m * bins + start, rows)],
                    k_ref.at[pl.ds(m * bins + n * rows, rows)],
                    k_sem.at[2 * n + m],
                )
            )
        w_copies.append(pltpu.make_async_copy(w_hbm.at[pl.ds(start, rows)], w_ref.at[here], w_sem.at[n]))
    h_copy = pltpu.make_async_copy(h_hbm, h_ref, h_sem)
    for copy in k_copies + w_copies + [h_copy]:
        copy.start()

    a_copy.wait()
    wide[8 : 8 + a_ref.shape[0], :] = a_ref[...].astype(f32)
    wide[6:8, :] = halo_ref[0:2, :]
    wide[8 + a_ref.shape[0] : 10 + a_ref.shape[0], :] = halo_ref[2:4, :]
    stride = HOP // LANES

    def build(t):
        for j in range(2 * HOP // LANES):
            strip = wide[pl.ds(6 + j + t * stride, 512, stride=stride), :]
            frame[t : t + 512, j * LANES : (j + 1) * LANES] = strip.astype(bf16)

    build(0)
    waited = 0
    for lo, hi in blocks:
        while waited < -(-hi // rows):
            k_copies[2 * waited].wait()
            k_copies[2 * waited + 1].wait()
            waited += 1
        for t in range(0, frames, 512):
            if lo == 0 and t + 512 < frames:
                build(t + 512)
            f = frame[t : t + 512, :]
            re = dot_nt(k_ref[lo:hi, :], f)
            im = dot_nt(k_ref[bins + lo : bins + hi, :], f)
            p_ref[lo:hi, t : t + 512] = (re * re + im * im).astype(bf16)

    for copy in w_copies + [h_copy]:
        copy.wait()
    wt[...] = w_ref[...].T
    inv = inverse(jnp.sum(wt[...].astype(f32), axis=1, keepdims=True))
    for t in range(0, frames, TILE):
        tile = slice(t, t + TILE)
        h = h_ref[:, tile]
        numer = None
        for lo, hi in blocks:
            model = dot(w_ref[lo:hi, :], h)
            ratio = (p_ref[lo:hi, tile].astype(f32) * inverse(model)).astype(bf16)
            part = dot(wt[:, lo:hi], ratio)
            numer = part if numer is None else numer + part
        new_ref[:, tile] = (h.astype(f32) * numer * inv).astype(bf16)


def template_kernel(size, p_base, w_base, extras, p_ref, w_ref, h_ref, *outs):
    frames = h_ref.shape[1]
    outs = list(outs)
    numw_ref = outs.pop(0)
    for lo, hi in row_blocks(size):
        w = w_ref[w_base + lo : w_base + hi, :]
        acc = None
        for t in range(0, frames, SPAN):
            h = h_ref[:, t : t + SPAN]
            model = dot(w, h)
            p = p_ref[p_base + lo : p_base + hi, t : t + SPAN]
            ratio = (p.astype(f32) * inverse(model)).astype(bf16)
            part = dot_nt(ratio, h)
            acc = part if acc is None else acc + part
        numw_ref[lo:hi, :] = acc.astype(numw_ref.dtype)
    if "send" in extras or "totals" in extras:
        total = dot_nt(jnp.ones((16, frames), bf16), h_ref[...])
        high = total.astype(bf16).astype(f32)
        low = (total - high).astype(bf16).astype(f32)
        if "send" in extras:
            row = lax.broadcasted_iota(jnp.int32, total.shape, 0)
            both = jnp.where(row == 0, high, jnp.where(row == 1, low, 0.0))
            numw_ref[size : size + 16, :] = both.astype(bf16)
        else:
            outs.pop(0)[...] = (high + low)[:8]
    if "templates" in extras:
        outs.pop(0)[...] = w_ref[w_base : w_base + size, :]


def activation_kernel(first, base, p_ref, w_ref, h_ref, *refs):
    if first:
        numer_ref, col_ref, wt = refs
    else:
        old_ref, oldcol_ref, new_ref, wt = refs
    frames = h_ref.shape[1]
    wt[...] = w_ref[...].T
    col = jnp.sum(wt[...].astype(f32), axis=1, keepdims=True)
    if first:
        col_ref[...] = jnp.broadcast_to(col, col_ref.shape)
    else:
        inv = inverse(col + oldcol_ref[:, :1])
    for t in range(0, frames, TILE):
        tile = slice(t, t + TILE)
        h = h_ref[:, tile]
        numer = None if first else old_ref[:, tile]
        for lo, hi in row_blocks(w_ref.shape[0]):
            model = dot(w_ref[lo:hi, :], h)
            p = p_ref[base + lo : base + hi, tile]
            ratio = (p.astype(f32) * inverse(model)).astype(bf16)
            part = dot(wt[:, lo:hi], ratio)
            numer = part if numer is None else numer + part
        if first:
            numer_ref[:, tile] = numer
        else:
            new_ref[:, tile] = (h.astype(f32) * numer * inv).astype(bf16)


def place_kernel(rows, at_ref, own_ref, acts_ref, out_ref, acts_out_ref, sems):
    copies = [pltpu.make_async_copy(acts_ref, acts_out_ref, sems.at[at_ref.shape[0]])]
    copies[0].start()
    for n in range(at_ref.shape[0]):
        start = pl.multiple_of(at_ref[n] * rows, 16)
        source = own_ref.at[pl.ds(n * rows, rows)]
        copies.append(pltpu.make_async_copy(source, out_ref.at[pl.ds(start, rows)], sems.at[n]))
        copies[-1].start()
    for copy in copies:
        copy.wait()


def place_other_kernel(rows, at_ref, other_ref, half_ref, out_ref, sems):
    copies = []
    for n in range(at_ref.shape[0]):
        start = pl.multiple_of(at_ref[n] * rows, 16)
        source = other_ref.at[pl.ds(n * rows, rows)]
        copies.append(pltpu.make_async_copy(source, out_ref.at[pl.ds(start, rows)], sems.at[n]))
        copies[-1].start()
    for copy in copies:
        copy.wait()


VMEM = pl.BlockSpec(memory_space=pltpu.VMEM)
HBM = pl.BlockSpec(memory_space=pltpu.HBM)
SMEM = pl.BlockSpec(memory_space=pltpu.SMEM)
ANY = pl.BlockSpec(memory_space=pl.ANY)


def call(kernel, outs, scratch, flops, *args, specs=None, out_spec=None, aliases={}, mib=16):
    size = sum(a.size * a.dtype.itemsize for a in args)
    size += sum(o.size * o.dtype.itemsize for o in outs)
    return pl.pallas_call(
        kernel,
        out_shape=tuple(outs),
        in_specs=specs or [VMEM] * len(args),
        out_specs=tuple([out_spec or VMEM] * len(outs)),
        scratch_shapes=scratch,
        input_output_aliases=aliases,
        cost_estimate=pl.CostEstimate(flops=flops, bytes_accessed=size, transcendentals=0),
        compiler_params=pltpu.CompilerParams(vmem_limit_bytes=mib * 1024 * 1024),
    )(*args)


def shape(dims, dtype):
    return jax.ShapeDtypeStruct(dims, dtype)


def analyse(at, audio, halo, kernel, weights, acts):
    bins, comps = weights.shape
    frames = acts.shape[1]
    blocks = at.shape[0]
    return call(
        functools.partial(analyse_kernel, bins // blocks),
        [shape((bins, frames), bf16), shape((comps, frames), bf16), shape((bins, comps), bf16)],
        [
            pltpu.VMEM(audio.shape, bf16),
            pltpu.VMEM(kernel.shape, bf16),
            pltpu.VMEM(acts.shape, bf16),
            pltpu.VMEM((audio.shape[0] + 16, LANES), f32),
            pltpu.VMEM((frames, 2 * HOP), bf16),
            pltpu.VMEM((comps, bins), bf16),
            pltpu.SemaphoreType.DMA,
            pltpu.SemaphoreType.DMA((2 * blocks,)),
            pltpu.SemaphoreType.DMA((blocks,)),
            pltpu.SemaphoreType.DMA,
        ],
        2 * bins * frames * (4 * HOP + 2 * comps),
        at, halo, *[pltpu.with_memory_space_constraint(x, pltpu.HBM) for x in (audio, kernel, weights, acts)],
        specs=[SMEM, VMEM, HBM, HBM, HBM, HBM],
        mib=32,
    )


def template_numerator(size, power, p_base, weights, w_base, acts, extras):
    comps = acts.shape[0]
    outs = [shape((size + 16, comps), bf16) if "send" in extras else shape((size, comps), f32)]
    if "totals" in extras:
        outs.append(shape((8, comps), f32))
    if "templates" in extras:
        outs.append(shape((size, comps), bf16))
    kernel = functools.partial(template_kernel, size, p_base, w_base, extras)
    return call(kernel, outs, [], 4 * size * acts.size, power, weights, acts)


def activation_numerator(power, base, weights, acts):
    size, comps = weights.shape
    return call(
        functools.partial(activation_kernel, True, base),
        [shape(acts.shape, f32), shape((comps, 128), f32)],
        [pltpu.VMEM((comps, size), bf16)],
        4 * size * acts.size, power, weights, acts,
    )


def new_activations(power, base, weights, acts, numer, colsum):
    size, comps = weights.shape
    return call(
        functools.partial(activation_kernel, False, base),
        [shape(acts.shape, bf16)],
        [pltpu.VMEM((comps, size), bf16)],
        4 * size * acts.size, power, weights, acts, numer, colsum,
    )[0]


def halo_rows(audio, peers):
    me = lax.axis_index("tm")
    odd = me % 2 == 1
    rows = HALF // LANES
    head, tail = audio[:rows], audio[audio.shape[0] - rows :]
    inner = [(i, i ^ 1) for i in range(peers)]
    outer = [(i, (i + 1) % peers if i % 2 else (i - 1) % peers) for i in range(peers)]
    one = lax.ppermute(jnp.where(odd, head, tail), "tm", inner)
    two = lax.ppermute(jnp.where(odd, tail, head), "tm", outer)
    two = jnp.where((me == 0) | (me == peers - 1), jnp.zeros_like(two), two)
    left = jnp.where(odd, one, two)
    right = jnp.where(odd, two, one)
    return jnp.concatenate([left, right], axis=0).astype(f32)


class Group:
    def __init__(self, bits, peers):
        me = lax.axis_index("tm")
        self.size = 1 << len(bits)
        self.me = sum(((me // b) % 2) << j for j, b in enumerate(bits))
        self.others = []
        for code in range(1, self.size):
            mask = sum(b for j, b in enumerate(bits) if code >> j & 1)
            self.others.append((code, [(i, i ^ mask) for i in range(peers)]))


def groups_of(peers):
    bits = [1 << b for b in range(peers.bit_length() - 1)]
    return Group(bits[:1], peers), Group(bits[1:3], peers), [Group([b], peers) for b in bits[3:]]


def halves_of(totals):
    hi = totals.astype(bf16)
    lo = (totals - hi.astype(f32)).astype(bf16)
    return (hi, lo), hi.astype(f32) + lo.astype(f32)


def swap(send, halves, perm):
    if halves is None:
        return lax.ppermute(send, "tm", perm), None
    rows = send.shape[0]
    pad = jnp.zeros((14, send.shape[1]), bf16)
    got = lax.ppermute(jnp.concatenate([send, halves[0][None], halves[1][None], pad], axis=0), "tm", perm)
    return got[:rows], got[rows].astype(f32) + got[rows + 1].astype(f32)


def sum_chips(mine, others, total, quad, pairs, direct):
    halves = None
    if total is not None:
        halves, total = halves_of(total)
    perms = [perm for _, perm in quad.others]
    if direct:
        for other, perm in zip(others, perms):
            more, part = swap(other.astype(bf16), halves, perm)
            mine = mine + more.astype(f32)
            total = None if total is None else total + part
    else:
        rows = mine.shape[0]
        more = lax.ppermute(jnp.concatenate([others[0], others[2]]).astype(bf16), "tm", perms[0])
        far = (others[1] + more[rows:].astype(f32)).astype(bf16)
        mine = mine + more[:rows].astype(f32)
        mine = mine + lax.ppermute(far, "tm", perms[1]).astype(f32)
    for group in pairs:
        if total is not None:
            halves, total = halves_of(total)
        mine = mine.astype(bf16)
        more, part = swap(mine, halves, group.others[0][1])
        mine = mine.astype(f32) + more.astype(f32)
        total = None if total is None else total + part
    return mine, total


def spread(part, quad, direct):
    perms = [perm for _, perm in quad.others]
    if direct:
        return [part] + [lax.ppermute(part, "tm", perm) for perm in perms]
    rows = part.shape[0]
    far = lax.ppermute(part, "tm", perms[1])
    got = lax.ppermute(jnp.concatenate([part, far]), "tm", perms[0])
    return [part, got[:rows], far, got[rows:]]


def on_device(audio, kernel, templates, activations):
    peers = lax.axis_size("tm")
    bins = templates.shape[0]
    size = bins // 2
    audio = audio.reshape(audio.shape[0] // LANES, LANES)
    halo = halo_rows(audio, peers)
    core, quad, pairs = groups_of(peers)
    rows = size // quad.size
    cuts = [0, rows // 2 // 16 * 16, rows]
    order = [quad.me] + [quad.me ^ code for code, _ in quad.others]
    at = [core.me * quad.size + q for q in order] + [(1 - core.me) * quad.size + q for q in order]
    at = jnp.stack(at).astype(jnp.int32)
    power, acts, weights = analyse(at, audio, halo, kernel, templates, activations)
    own_w, other_w, base = weights, weights, size
    for step in range(ITERS):
        last = step == ITERS - 1
        (send,) = template_numerator(size, power, size, other_w, base, acts, ("send",))
        got = lax.ppermute(send, "tm", core.others[0][1])
        rest, total = template_numerator(size - rows, power, rows, own_w, rows, acts, ("totals",))
        mine, weights = template_numerator(rows, power, 0, own_w, 0, acts, ("templates",))
        rest = rest + got[rows:size].astype(f32)
        mine = mine + got[:rows].astype(f32)
        total = total[0] + (got[size].astype(f32) + got[size + 1].astype(f32))
        pieces, rowsum = [], None
        for lo, hi in zip(cuts[:-1], cuts[1:]):
            others = [rest[n * rows + lo : n * rows + hi] for n in range(quad.size - 1)]
            part, tot = sum_chips(
                mine[lo:hi], others, total if lo == 0 else None, quad, pairs, DIRECT[0][lo == 0]
            )
            rowsum = tot if lo == 0 else rowsum
            part = (weights[lo:hi].astype(f32) * part / rowsum[None, :]).astype(bf16)
            pieces.append(spread(part, quad, DIRECT[1][lo == 0]))
        own_w = jnp.concatenate([piece[n] for n in range(quad.size) for piece in pieces], axis=0)
        other_w, base = lax.ppermute(own_w, "tm", core.others[0][1]), 0
        if not last:
            numer, colsum = activation_numerator(power, 0, own_w, acts)
            acts = new_activations(power, size, other_w, acts, numer, colsum)
    out, acts = call(
        functools.partial(place_kernel, rows),
        [shape(templates.shape, bf16), shape(acts.shape, bf16)],
        [pltpu.SemaphoreType.DMA((quad.size + 1,))],
        2 * acts.size * acts.shape[0],
        at[: quad.size], own_w, acts, specs=[SMEM, ANY, ANY], out_spec=ANY,
    )
    (out,) = call(
        functools.partial(place_other_kernel, rows),
        [shape(templates.shape, bf16)],
        [pltpu.SemaphoreType.DMA((quad.size,))],
        0,
        at[quad.size :], other_w, out, specs=[SMEM, ANY, ANY], out_spec=ANY, aliases={2: 0},
    )
    return (acts, out)


def solution(mesh):
    in_specs = (P(("groups", "tm")), P(), P(), P(None, ("groups", "tm")))
    out_specs = (P(None, ("groups", "tm")), P("groups", None))
    return jax.shard_map(
        on_device, mesh=mesh, in_specs=in_specs, out_specs=out_specs, check_vma=False
    )
```
